256 devices in a mesh: row: 8 (over x, core), col: 32 (over z, y).
Axes of the slice: x: 4, y: 4, z: 8, core: 2. Of those that a mesh axis runs over, the one named last changes fastest.
Arguments:
- base_mttkrp: float32 [512, 128], P('row'), may hold values from -6 to 6
- operator_b: bfloat16 [512, 8192, 128], P('row', 'col'), may hold values from -6 to 6
- operator_c: bfloat16 [512, 8192, 128], P('row', 'col'), may hold values from -6 to 6
- delta_b: bfloat16 [8192, 128], P('col', 'row'), may hold values from -0.0625 to 0.0625
- delta_c: bfloat16 [8192, 128], P('col', 'row'), may hold values from -0.0625 to 0.0625
- factor_b: float32 [8192, 128], P('col', 'row'), may hold values from 0 to 2
- factor_c: float32 [8192, 128], P('col', 'row'), may hold values from 0 to 2
Outputs:
- factor_a: float32 [512, 128], P('row')
- gram_next: float32 [128, 128], replicated
The draws below stay inside these ranges and needn't reach their ends.
All inputs are finite; a program needn't handle non-finite values.
Results may differ from the reference program's by a relative error of at most 0.0003.
Values may be sent and summed in bfloat16 or wider, within the bound.
A program may use at most 64 MiB of HBM per device.

```python
import jax
import jax.numpy as jnp
from jax import lax

R = 128
J = 8192
K = 8192
ROWS = 512


def block_levels(own_key, dims, cuts, least, high):
    gain, own = 1.0, jax.random.fold_in(own_key, 6)
    for axis_at, shards_of in cuts:
        steps = jnp.exp(jax.random.uniform(jax.random.fold_in(own, axis_at), (shards_of,), jnp.float32, least / len(cuts), high / len(cuts)))
        gain = gain * jnp.repeat(steps, dims[axis_at] // shards_of).reshape([-1 if axis == axis_at else 1 for axis in range(len(dims))])
    return gain


def scatter_about(stream_key, dims, spread, reach, split=(), kind=jnp.bfloat16):
    factor_of = block_levels(stream_key, dims, split, -0.22, 0.18) if split else 1.0
    array = jax.random.normal(stream_key, dims, jnp.float32) * spread * factor_of
    return jnp.minimum(jnp.maximum(array, -reach), reach).astype(kind)


def setup_inputs(seed: int = 0) -> dict:
    seeds = jax.random.split(jax.random.key(seed), 8)
    base_mttkrp = scatter_about(seeds[0], (ROWS, R), 1.0, 6.0, ((0, 8),), jnp.float32)
    operator_b = scatter_about(seeds[1], (ROWS, J, R), 1.0, 6.0, ((0, 8), (1, 32)))
    operator_c = scatter_about(seeds[2], (ROWS, K, R), 1.0, 6.0, ((0, 8), (1, 32)))
    delta_b = scatter_about(seeds[3], (J, R), J ** -0.5, 0.0625, ((0, 32), (1, 8)))
    delta_c = scatter_about(seeds[4], (K, R), K ** -0.5, 0.0625, ((0, 32), (1, 8)))
    factor_b = jnp.clip(2.0 * jax.random.uniform(seeds[5], (J, R), jnp.float32) ** block_levels(seeds[5], (J, R), ((0, 32), (1, 8)), -0.2, 0.2), 0.0, 2.0)
    factor_c = jnp.clip(2.0 * jax.random.uniform(seeds[6], (K, R), jnp.float32) ** block_levels(seeds[6], (K, R), ((0, 32), (1, 8)), -0.2, 0.2), 0.0, 2.0)
    return dict(base_mttkrp=base_mttkrp, operator_b=operator_b, operator_c=operator_c, delta_b=delta_b, delta_c=delta_c, factor_b=factor_b, factor_c=factor_c)


def contract_block(operators, deltas):
    block_b, block_c = operators
    delta_b, delta_c = deltas
    part_b = jnp.einsum('ijr,jr->ir', block_b.astype(jnp.float32), delta_b.astype(jnp.float32), precision=lax.Precision.HIGHEST)
    part_c = jnp.einsum('ijr,jr->ir', block_c.astype(jnp.float32), delta_c.astype(jnp.float32), precision=lax.Precision.HIGHEST)
    return part_b + part_c

def solve_rows(mttkrp, hadamard):
    lower = jnp.linalg.cholesky(hadamard)
    inner = jax.scipy.linalg.solve_triangular(lower, mttkrp.T, lower=True)
    return jax.scipy.linalg.solve_triangular(lower, inner, lower=True, trans=1).T

def reference(base_mttkrp, operator_b, operator_c, delta_b, delta_c, factor_b, factor_c):
    blocks = ROWS // 32
    shaped_b = operator_b.reshape(blocks, 32, J, R)
    shaped_c = operator_c.reshape(blocks, 32, K, R)
    contraction = lax.map(lambda pair: contract_block(pair, (delta_b, delta_c)), (shaped_b, shaped_c))
    mttkrp = base_mttkrp + contraction.reshape(ROWS, R)
    gram_b = jnp.dot(factor_b.T, factor_b, precision=lax.Precision.HIGHEST)
    gram_c = jnp.dot(factor_c.T, factor_c, precision=lax.Precision.HIGHEST)
    hadamard = gram_b / J * (gram_c / K)
    factor_a = solve_rows(mttkrp, hadamard)
    gram_a = jnp.dot(factor_a.T, factor_a, precision=lax.Precision.HIGHEST)
    gram_next = gram_a / ROWS * (gram_c / K)
    return (factor_a, gram_next)
```

```python
import functools

import jax
import jax.numpy as jnp
from jax import lax
from jax.experimental import pallas as pl
from jax.experimental.pallas import tpu as pltpu
from jax.sharding import PartitionSpec as P

J = 8192
K = 8192
ROWS = 512
R = 128
F32 = jnp.float32
BF16 = jnp.bfloat16
HIGH = lax.Precision.HIGHEST
MESH = pl.DeviceIdType.MESH

NX, NC, NY, NZ = 4, 2, 4, 8
ROW_OFFS = [(dx, dc) for dx in range(NX) for dc in range(NC) if dx or dc]
XY_OFFS = [(dx, dc, dy) for dy in range(NY) for dx in range(NX) for dc in range(NC) if dx or dc or dy]
GROUPS = 8


def lane_bcast(v, lane):
    return jnp.broadcast_to(v[:, lane : lane + 1], (8, R))


def sub_bcast(v, sub):
    return jnp.broadcast_to(v[sub : sub + 1, :], (8, R))


def invert(A):
    lane = lax.broadcasted_iota(jnp.int32, (8, R), 1)
    sub = lax.broadcasted_iota(jnp.int32, (8, R), 0)
    A = list(A)
    for p in range(16):
        l0 = 8 * p
        inside = (lane >= l0) & (lane < l0 + 8)
        c = [lane_bcast(A[p], l0 + i) for i in range(8)]
        rows = jnp.where(inside, jnp.where(lane - l0 == sub, 1.0, 0.0), A[p])
        for i in range(8):
            rinv = 1.0 / sub_bcast(c[i], i)
            pivot = sub_bcast(rows, i) * rinv
            rows = jnp.where(sub == i, pivot, rows - c[i] * pivot)
            for m in range(i + 1, 8):
                dr = sub_bcast(c[m], i) * rinv
                c[m] = jnp.where(sub == i, dr, c[m] - c[i] * dr)
        each = [sub_bcast(rows, i) for i in range(8)]
        for m in [(p + 1 + t) % 16 for t in range(15)]:
            a = A[m]
            t = [lane_bcast(a, l0 + i) * each[i] for i in range(8)]
            s = ((t[0] + t[1]) + (t[2] + t[3])) + ((t[4] + t[5]) + (t[6] + t[7]))
            A[m] = jnp.where(inside, 0.0, a) - s
        A[p] = rows
    return A


def kernel(
    base, opb, opc, db, dc, fb, fc, fa_out, gn_out,
    bv, cv, st_f, rv_f, rv_d, part_g, y_g, z_g, ag_g, part_m, y_m, z_m, ag_m, inv,
    op_sem, f_s, f_r, d_s, d_r, yg_s, yg_r, zg_s, zg_r, ag_s, ag_r, ym_s, ym_r, zm_s, zm_r, am_s, am_r,
):
    r, c = lax.axis_index("row"), lax.axis_index("col")
    x, core = r // 2, lax.rem(r, 2)
    z, y = c // NY, lax.rem(c, NY)

    def at_row(dx, dcore):
        return lax.rem(x + dx, NX) * 2 + lax.rem(core + dcore, NC)

    def at_col(dz, dy):
        return lax.rem(z + dz, NZ) * NY + lax.rem(y + dy, NY)

    def remote(src, dst, ss, rs, k, row, col):
        return pltpu.make_async_remote_copy(
            src_ref=src, dst_ref=dst, send_sem=ss.at[k], recv_sem=rs.at[k],
            device_id=(row, col), device_id_type=MESH)

    loads = []
    for g in range(GROUPS):
        rows = pl.ds(8 * g, 8)
        loads.append((pltpu.make_async_copy(opb.at[rows], bv.at[rows], op_sem.at[0, g]),
                      pltpu.make_async_copy(opc.at[rows], cv.at[rows], op_sem.at[1, g])))

    barrier = pltpu.get_barrier_semaphore()
    for dz in range(1, NZ):
        pl.semaphore_signal(barrier, inc=1, device_id=(r, at_col(dz, 0)), device_id_type=MESH)
    for dx, dcore, dy in reversed(XY_OFFS):
        pl.semaphore_signal(barrier, inc=1, device_id=(at_row(dx, dcore), at_col(0, dy)), device_id_type=MESH)
    for pair in loads:
        for copy in pair:
            copy.start()
    st_f[0] = fb[...]
    st_f[1] = fc[...]
    rv_d[r, :, 0:256] = db[...]
    rv_d[r, :, 256:512] = dc[...]
    rv_f[r] = st_f[core]
    pl.semaphore_wait(barrier, NZ - 1 + len(XY_OFFS))

    sent = []
    send_f, send_d = [], []
    for k, (dx, dcore) in enumerate(ROW_OFFS):
        send_f.append(remote(st_f.at[lax.rem(core + dcore, NC)], rv_f.at[r], f_s, f_r, k, at_row(dx, dcore), c))
        send_f[-1].start()
    for k, (dx, dcore) in enumerate(ROW_OFFS):
        send_d.append(remote(rv_d.at[r], rv_d.at[r], d_s, d_r, k, at_row(dx, dcore), c))
        send_d[-1].start()
    sent += send_f + send_d

    for copy in send_f:
        copy.wait_recv()
    mine = rv_f[pl.ds(2 * x, 2)].reshape(32, 256)
    gram = lax.dot_general(mine, rv_f[...].reshape(R, 256), (((1,), (1,)), ((), ())),
                           precision=HIGH, preferred_element_type=F32)
    part_g[...] = gram.reshape(NY, 8, R)
    send_yg = []
    for dy in range(1, NY):
        send_yg.append(remote(part_g.at[lax.rem(y + dy, NY)], y_g.at[dy - 1], yg_s, yg_r, dy - 1, r, at_col(0, dy)))
        send_yg[-1].start()

    for copy in send_d:
        copy.wait_recv()
    eye = lax.broadcasted_iota(jnp.int32, (R, R), 0) == lax.broadcasted_iota(jnp.int32, (R, R), 1)

    def contract(g):
        for copy in loads[g]:
            copy.wait()
        d_b = rv_d[:, :, 0:256].reshape(R, 256)
        d_c = rv_d[:, :, 256:512].reshape(R, 256)
        found = []
        for i in range(8 * g, 8 * g + 8):
            both = jnp.dot(d_b, bv[i], preferred_element_type=F32)
            both = both + jnp.dot(d_c, cv[i], preferred_element_type=F32)
            found.append(jnp.sum(jnp.where(eye, both, 0.0), axis=0, keepdims=True))
        part_m[g // 2, pl.ds(8 * (g % 2), 8), :] = jnp.concatenate(found, axis=0)

    for g in range(GROUPS // 2):
        contract(g)

    for copy in send_yg:
        copy.wait_recv()
    z_g[z] = (part_g[y] + y_g[0]) + (y_g[1] + y_g[2])
    send_zg = []
    for dz in range(1, NZ):
        send_zg.append(remote(z_g.at[z], z_g.at[z], zg_s, zg_r, dz - 1, r, at_col(dz, 0)))
        send_zg[-1].start()

    for g in range(GROUPS // 2, GROUPS):
        contract(g)
    send_ym = []
    for dy in range(1, NY):
        send_ym.append(remote(part_m.at[lax.rem(y + dy, NY)], y_m.at[dy - 1], ym_s, ym_r, dy - 1, r, at_col(0, dy)))
        send_ym[-1].start()

    for copy in send_zg:
        copy.wait_recv()
    ag_g[r, y] = ((z_g[0] + z_g[1]) + (z_g[2] + z_g[3])) + ((z_g[4] + z_g[5]) + (z_g[6] + z_g[7]))
    send_ag = []
    for k, (dx, dcore, dy) in enumerate(XY_OFFS):
        send_ag.append(remote(ag_g.at[r, y], ag_g.at[r, y], ag_s, ag_r, k, at_row(dx, dcore), at_col(0, dy)))
        send_ag[-1].start()

    for copy in send_ym:
        copy.wait_recv()
    z_m[z] = (part_m[y] + y_m[0]) + (y_m[1] + y_m[2])
    send_zm = []
    for dz in range(1, NZ):
        send_zm.append(remote(z_m.at[z], z_m.at[z], zm_s, zm_r, dz - 1, r, at_col(dz, 0)))
        send_zm[-1].start()
    for copy in send_zm:
        copy.wait_recv()
    summed = ((z_m[0] + z_m[1]) + (z_m[2] + z_m[3])) + ((z_m[4] + z_m[5]) + (z_m[6] + z_m[7]))
    ag_m[r, y] = base[pl.ds(pl.multiple_of(16 * y, 16), 16), :] + summed
    send_am = []
    for k, (dx, dcore, dy) in enumerate(XY_OFFS):
        send_am.append(remote(ag_m.at[r, y], ag_m.at[r, y], am_s, am_r, k, at_row(dx, dcore), at_col(0, dy)))
        send_am[-1].start()

    for copy in send_ag:
        copy.wait_recv()
    gathered = ag_g[...].reshape(NX, NC, 32, R)
    gram_b = gathered[:, 0].reshape(R, R)
    gram_c = gathered[:, 1].reshape(R, R) / K
    hadamard = gram_b / J * gram_c
    blocks = invert([hadamard[8 * m : 8 * m + 8, :] for m in range(16)])
    for m in range(16):
        inv[8 * m : 8 * m + 8, :] = blocks[m]

    for copy in send_am:
        copy.wait_recv()
    whole = ag_m[...].reshape(ROWS, R)
    mtm = lax.dot_general(whole, whole, (((0,), (0,)), ((), ())), precision=HIGH, preferred_element_type=F32)
    inverse = inv[...]
    own = ag_m[r].reshape(64, R)
    fa_out[...] = jnp.dot(own, inverse, precision=HIGH, preferred_element_type=F32)
    half = jnp.dot(mtm, inverse, precision=HIGH, preferred_element_type=F32)
    gram_a = lax.dot_general(inverse, half, (((0,), (0,)), ((), ())), precision=HIGH, preferred_element_type=F32)
    gn_out[...] = gram_a / ROWS * gram_c

    for copy in sent + send_yg + send_zg + send_ag + send_ym + send_zm + send_am:
        copy.wait_send()


def shards(base_mttkrp, operator_b, operator_c, delta_b, delta_c, factor_b, factor_c):
    vmem = pl.BlockSpec(memory_space=pltpu.VMEM)
    hbm = pl.BlockSpec(memory_space=pl.ANY)

    def sems(*counts):
        return [pltpu.SemaphoreType.DMA((n,)) for n in counts for _ in range(2)]

    return pl.pallas_call(
        kernel,
        out_shape=(jax.ShapeDtypeStruct((64, R), F32), jax.ShapeDtypeStruct((R, R), F32)),
        in_specs=[vmem, hbm, hbm, vmem, vmem, vmem, vmem],
        out_specs=(vmem, vmem),
        scratch_shapes=[
            pltpu.VMEM((64, 256, R), BF16),
            pltpu.VMEM((64, 256, R), BF16),
            pltpu.VMEM((2, 16, 256), F32),
            pltpu.VMEM((8, 16, 256), F32),
            pltpu.VMEM((8, 16, 512), BF16),
            pltpu.VMEM((NY, 8, R), F32),
            pltpu.VMEM((NY - 1, 8, R), F32),
            pltpu.VMEM((NZ, 8, R), F32),
            pltpu.VMEM((8, NY, 8, R), F32),
            pltpu.VMEM((NY, 16, R), F32),
            pltpu.VMEM((NY - 1, 16, R), F32),
            pltpu.VMEM((NZ, 16, R), F32),
            pltpu.VMEM((8, NY, 16, R), F32),
            pltpu.VMEM((R, R), F32),
            pltpu.SemaphoreType.DMA((2, GROUPS)),
        ] + sems(7, 7, 3, 7, 31, 3, 7, 31),
        compiler_params=pltpu.CompilerParams(
            collective_id=0, has_side_effects=True, vmem_limit_bytes=48 * 2**20),
        name="update",
    )(base_mttkrp, operator_b, operator_c, delta_b.T, delta_c.T, factor_b.T, factor_c.T)


def solution(mesh):
    return jax.shard_map(
        shards,
        mesh=mesh,
        in_specs=(
            P("row", None),
            P("row", "col", None),
            P("row", "col", None),
            P("col", "row"),
            P("col", "row"),
            P("col", "row"),
            P("col", "row"),
        ),
        out_specs=(P("row", None), P()),
        check_vma=False,
    )
```

```python
import functools

import jax
import jax.numpy as jnp
from jax import lax
from jax.experimental import pallas as pl
from jax.experimental.pallas import tpu as pltpu
from jax.sharding import PartitionSpec as P

J = 8192
K = 8192
ROWS = 512
R = 128
F32 = jnp.float32
BF16 = jnp.bfloat16
HIGH = lax.Precision.HIGHEST
MESH = pl.DeviceIdType.MESH

NX, NC, NY, NZ = 4, 2, 4, 8
ROW_OFFS = [(dx, dc) for dx in range(NX) for dc in range(NC) if dx or dc]
XY_OFFS = [(dx, dc, dy) for dy in range(NY) for dx in range(NX) for dc in range(NC) if dx or dc or dy]
GROUPS = 8


def lane_bcast(v, lane):
    return jnp.broadcast_to(v[:, lane : lane + 1], (8, R))


def sub_bcast(v, sub):
    return jnp.broadcast_to(v[sub : sub + 1, :], (8, R))


def invert(A):
    lane = lax.broadcasted_iota(jnp.int32, (8, R), 1)
    sub = lax.broadcasted_iota(jnp.int32, (8, R), 0)
    A = list(A)
    for p in range(16):
        l0 = 8 * p
        inside = (lane >= l0) & (lane < l0 + 8)
        c = [lane_bcast(A[p], l0 + i) for i in range(8)]
        rows = jnp.where(inside, jnp.where(lane - l0 == sub, 1.0, 0.0), A[p])
        for i in range(8):
            rinv = 1.0 / sub_bcast(c[i], i)
            pivot = sub_bcast(rows, i) * rinv
            rows = jnp.where(sub == i, pivot, rows - c[i] * pivot)
            for m in range(i + 1, 8):
                dr = sub_bcast(c[m], i) * rinv
                c[m] = jnp.where(sub == i, dr, c[m] - c[i] * dr)
        each = [sub_bcast(rows, i) for i in range(8)]
        for m in [(p + 1 + t) % 16 for t in range(15)]:
            a = A[m]
            t = [lane_bcast(a, l0 + i) * each[i] for i in range(8)]
            s = ((t[0] + t[1]) + (t[2] + t[3])) + ((t[4] + t[5]) + (t[6] + t[7]))
            A[m] = jnp.where(inside, 0.0, a) - s
        A[p] = rows
    return A


def kernel(
    base, opb, opc, db, dc, fb, fc, fa_out, gn_out,
    bv, cv, st_f, rv_f, rv_d, part_g, y_g, z_g, ag_g, part_m, y_m, z_m, ag_m, inv,
    base_v, in_sem, op_sem, f_s, f_r, d_s, d_r, yg_s, yg_r, zg_s, zg_r, ag_s, ag_r, ym_s, ym_r, zm_s, zm_r, am_s, am_r,
):
    r, c = lax.axis_index("row"), lax.axis_index("col")
    x, core = r // 2, lax.rem(r, 2)
    z, y = c // NY, lax.rem(c, NY)

    def at_row(dx, dcore):
        return lax.rem(x + dx, NX) * 2 + lax.rem(core + dcore, NC)

    def at_col(dz, dy):
        return lax.rem(z + dz, NZ) * NY + lax.rem(y + dy, NY)

    def remote(src, dst, ss, rs, k, row, col):
        return pltpu.make_async_remote_copy(
            src_ref=src, dst_ref=dst, send_sem=ss.at[k], recv_sem=rs.at[k],
            device_id=(row, col), device_id_type=MESH)

    loads = []
    for g in range(GROUPS):
        rows = pl.ds(8 * g, 8)
        loads.append((pltpu.make_async_copy(opb.at[rows], bv.at[rows], op_sem.at[0, g]),
                      pltpu.make_async_copy(opc.at[rows], cv.at[rows], op_sem.at[1, g])))

    small = [pltpu.make_async_copy(src, dst, in_sem.at[k]) for k, (src, dst) in enumerate((
        (fb, st_f.at[0]), (fc, st_f.at[1]), (db, rv_d.at[r, :, pl.ds(0, 256)]),
        (dc, rv_d.at[r, :, pl.ds(256, 256)]), (base, base_v)))]
    for copy in small:
        copy.start()
    barrier = pltpu.get_barrier_semaphore()
    for dz in range(1, NZ):
        pl.semaphore_signal(barrier, inc=1, device_id=(r, at_col(dz, 0)), device_id_type=MESH)
    for dx, dcore, dy in reversed(XY_OFFS):
        pl.semaphore_signal(barrier, inc=1, device_id=(at_row(dx, dcore), at_col(0, dy)), device_id_type=MESH)
    for pair in loads:
        for copy in pair:
            copy.start()
    for copy in small:
        copy.wait()
    rv_f[r] = st_f[core]
    pl.semaphore_wait(barrier, NZ - 1 + len(XY_OFFS))

    sent = []
    send_f, send_d = [], []
    for k, (dx, dcore) in enumerate(ROW_OFFS):
        send_f.append(remote(st_f.at[lax.rem(core + dcore, NC)], rv_f.at[r], f_s, f_r, k, at_row(dx, dcore), c))
        send_f[-1].start()
    for k, (dx, dcore) in enumerate(ROW_OFFS):
        send_d.append(remote(rv_d.at[r], rv_d.at[r], d_s, d_r, k, at_row(dx, dcore), c))
        send_d[-1].start()
    sent += send_f + send_d

    for copy in send_f:
        copy.wait_recv()
    mine = rv_f[pl.ds(2 * x, 2)].reshape(32, 256)
    gram = lax.dot_general(mine, rv_f[...].reshape(R, 256), (((1,), (1,)), ((), ())),
                           precision=HIGH, preferred_element_type=F32)
    part_g[...] = gram.reshape(NY, 8, R)
    send_yg = []
    for dy in range(1, NY):
        send_yg.append(remote(part_g.at[lax.rem(y + dy, NY)], y_g.at[dy - 1], yg_s, yg_r, dy - 1, r, at_col(0, dy)))
        send_yg[-1].start()

    for copy in send_d:
        copy.wait_recv()
    eye = lax.broadcasted_iota(jnp.int32, (R, R), 0) == lax.broadcasted_iota(jnp.int32, (R, R), 1)

    def contract(g):
        for copy in loads[g]:
            copy.wait()
        d_b = rv_d[:, :, 0:256].reshape(R, 256)
        d_c = rv_d[:, :, 256:512].reshape(R, 256)
        found = []
        for i in range(8 * g, 8 * g + 8):
            both = jnp.dot(d_b, bv[i], preferred_element_type=F32)
            both = both + jnp.dot(d_c, cv[i], preferred_element_type=F32)
            found.append(jnp.sum(jnp.where(eye, both, 0.0), axis=0, keepdims=True))
        part_m[g // 2, pl.ds(8 * (g % 2), 8), :] = jnp.concatenate(found, axis=0)

    for g in range(GROUPS // 2):
        contract(g)

    for copy in send_yg:
        copy.wait_recv()
    z_g[z] = (part_g[y] + y_g[0]) + (y_g[1] + y_g[2])
    send_zg = []
    for dz in range(1, NZ):
        send_zg.append(remote(z_g.at[z], z_g.at[z], zg_s, zg_r, dz - 1, r, at_col(dz, 0)))
        send_zg[-1].start()

    for g in range(GROUPS // 2, GROUPS):
        contract(g)
    send_ym = []
    for dy in range(1, NY):
        send_ym.append(remote(part_m.at[lax.rem(y + dy, NY)], y_m.at[dy - 1], ym_s, ym_r, dy - 1, r, at_col(0, dy)))
        send_ym[-1].start()

    for copy in send_zg:
        copy.wait_recv()
    ag_g[r, y] = ((z_g[0] + z_g[1]) + (z_g[2] + z_g[3])) + ((z_g[4] + z_g[5]) + (z_g[6] + z_g[7]))
    send_ag = []
    for k, (dx, dcore, dy) in enumerate(XY_OFFS):
        send_ag.append(remote(ag_g.at[r, y], ag_g.at[r, y], ag_s, ag_r, k, at_row(dx, dcore), at_col(0, dy)))
        send_ag[-1].start()

    for copy in send_ym:
        copy.wait_recv()
    z_m[z] = (part_m[y] + y_m[0]) + (y_m[1] + y_m[2])
    send_zm = []
    for dz in range(1, NZ):
        send_zm.append(remote(z_m.at[z], z_m.at[z], zm_s, zm_r, dz - 1, r, at_col(dz, 0)))
        send_zm[-1].start()
    for copy in send_zm:
        copy.wait_recv()
    summed = ((z_m[0] + z_m[1]) + (z_m[2] + z_m[3])) + ((z_m[4] + z_m[5]) + (z_m[6] + z_m[7]))
    ag_m[r, y] = base_v[pl.ds(pl.multiple_of(16 * y, 16), 16), :] + summed
    send_am = []
    for k, (dx, dcore, dy) in enumerate(XY_OFFS):
        send_am.append(remote(ag_m.at[r, y], ag_m.at[r, y], am_s, am_r, k, at_row(dx, dcore), at_col(0, dy)))
        send_am[-1].start()

    for copy in send_ag:
        copy.wait_recv()
    gathered = ag_g[...].reshape(NX, NC, 32, R)
    gram_b = gathered[:, 0].reshape(R, R)
    gram_c = gathered[:, 1].reshape(R, R) / K
    hadamard = gram_b / J * gram_c
    blocks = invert([hadamard[8 * m : 8 * m + 8, :] for m in range(16)])
    for m in range(16):
        inv[8 * m : 8 * m + 8, :] = blocks[m]

    for copy in send_am:
        copy.wait_recv()
    whole = ag_m[...].reshape(ROWS, R)
    mtm = lax.dot_general(whole, whole, (((0,), (0,)), ((), ())), precision=HIGH, preferred_element_type=F32)
    inverse = inv[...]
    own = ag_m[r].reshape(64, R)
    fa_out[...] = jnp.dot(own, inverse, precision=HIGH, preferred_element_type=F32)
    half = jnp.dot(mtm, inverse, precision=HIGH, preferred_element_type=F32)
    gram_a = lax.dot_general(inverse, half, (((0,), (0,)), ((), ())), precision=HIGH, preferred_element_type=F32)
    gn_out[...] = gram_a / ROWS * gram_c

    for copy in sent + send_yg + send_zg + send_ag + send_ym + send_zm + send_am:
        copy.wait_send()


def shards(base_mttkrp, operator_b, operator_c, delta_b, delta_c, factor_b, factor_c):
    vmem = pl.BlockSpec(memory_space=pltpu.VMEM)
    hbm = pl.BlockSpec(memory_space=pl.ANY)

    def sems(*counts):
        return [pltpu.SemaphoreType.DMA((n,)) for n in counts for _ in range(2)]

    return pl.pallas_call(
        kernel,
        out_shape=(jax.ShapeDtypeStruct((64, R), F32), jax.ShapeDtypeStruct((R, R), F32)),
        in_specs=[hbm] * 7,
        out_specs=(vmem, vmem),
        scratch_shapes=[
            pltpu.VMEM((64, 256, R), BF16),
            pltpu.VMEM((64, 256, R), BF16),
            pltpu.VMEM((2, 16, 256), F32),
            pltpu.VMEM((8, 16, 256), F32),
            pltpu.VMEM((8, 16, 512), BF16),
            pltpu.VMEM((NY, 8, R), F32),
            pltpu.VMEM((NY - 1, 8, R), F32),
            pltpu.VMEM((NZ, 8, R), F32),
            pltpu.VMEM((8, NY, 8, R), F32),
            pltpu.VMEM((NY, 16, R), F32),
            pltpu.VMEM((NY - 1, 16, R), F32),
            pltpu.VMEM((NZ, 16, R), F32),
            pltpu.VMEM((8, NY, 16, R), F32),
            pltpu.VMEM((R, R), F32),
            pltpu.VMEM((64, R), F32),
            pltpu.SemaphoreType.DMA((5,)),
            pltpu.SemaphoreType.DMA((2, GROUPS)),
        ] + sems(7, 7, 3, 7, 31, 3, 7, 31),
        compiler_params=pltpu.CompilerParams(
            collective_id=0, has_side_effects=True, vmem_limit_bytes=60 * 2**20),
        name="update",
    )(base_mttkrp, operator_b, operator_c, delta_b.T, delta_c.T, factor_b.T, factor_c.T)


def solution(mesh):
    return jax.shard_map(
        shards,
        mesh=mesh,
        in_specs=(
            P("row", None),
            P("row", "col", None),
            P("row", "col", None),
            P("col", "row"),
            P("col", "row"),
            P("col", "row"),
            P("col", "row"),
        ),
        out_specs=(P("row", None), P()),
        check_vma=False,
    )
```

```python
import functools

import jax
import jax.numpy as jnp
from jax import lax
from jax.experimental import pallas as pl
from jax.experimental.pallas import tpu as pltpu
from jax.sharding import PartitionSpec as P

J = 8192
K = 8192
ROWS = 512
R = 128
F32 = jnp.float32
BF16 = jnp.bfloat16
HIGH = lax.Precision.HIGHEST
MESH = pl.DeviceIdType.MESH

NX, NC, NY, NZ = 4, 2, 4, 8
ROW_OFFS = [(dx, dc) for dx in range(NX) for dc in range(NC) if dx or dc]
XY_OFFS = [(dx, dc, dy) for dy in range(NY) for dx in range(NX) for dc in range(NC) if dx or dc or dy]
GREETED = [(dx, dc, 0, 0) for dx, dc in reversed(ROW_OFFS)] + [(0, 0, dy, 0) for dy in (2, 1, 3)] + [(0, 0, 0, 1), (0, 0, 0, 7)]
GROUPS = 8


def lane_bcast(v, lane):
    return jnp.broadcast_to(v[:, lane : lane + 1], (8, R))


def sub_bcast(v, sub):
    return jnp.broadcast_to(v[sub : sub + 1, :], (8, R))


def invert(A):
    lane = lax.broadcasted_iota(jnp.int32, (8, R), 1)
    sub = lax.broadcasted_iota(jnp.int32, (8, R), 0)
    A = list(A)
    for p in range(R // 16):
        l0 = 16 * p
        inside = (lane >= l0) & (lane < l0 + 16)
        own = [2 * p, 2 * p + 1]
        ahead = [m for m in (2 * p + 2, 2 * p + 3) if m < 16]
        c = [[lane_bcast(A[u], l0 + i) for u in own] for i in range(16)]
        early = {m: [lane_bcast(A[m], l0 + i) for i in range(16)] for m in ahead}
        rows = [jnp.where(inside, jnp.where(lane - l0 == sub + 8 * k, 1.0, 0.0), A[u]) for k, u in enumerate(own)]
        for i in range(0, 16, 2):
            v, s = i // 8, i % 8
            a, b = sub_bcast(c[i][v], s), sub_bcast(c[i + 1][v], s)
            d, e = sub_bcast(c[i][v], s + 1), sub_bcast(c[i + 1][v], s + 1)
            det = 1.0 / (a * e - b * d)
            g0 = [(c[i][u] * e - c[i + 1][u] * d) * det for u in range(2)]
            g1 = [(c[i + 1][u] * a - c[i][u] * b) * det for u in range(2)]
            g0[v] = jnp.where(sub == s, -(e * det), jnp.where(sub == s + 1, d * det, g0[v]))
            g1[v] = jnp.where(sub == s, b * det, jnp.where(sub == s + 1, -(a * det), g1[v]))
            hit = (sub == s) | (sub == s + 1)

            def step(t):
                r0, r1 = sub_bcast(t[v], s), sub_bcast(t[v], s + 1)
                kept = [jnp.where(hit, 0.0, t[u]) if u == v else t[u] for u in range(2)]
                return [kept[u] - (g0[u] * r0 + g1[u] * r1) for u in range(2)]

            for m in range(i + 2, 16):
                c[m] = step(c[m])
            rows = step(rows)
        new = list(A)
        for m in ahead:
            t = [early[m][i] * sub_bcast(rows[i // 8], i % 8) for i in range(16)]
            while len(t) > 1:
                t = [t[q] + t[q + 1] for q in range(0, len(t), 2)]
            new[m] = jnp.where(inside, 0.0, A[m]) - t[0]
        padded = jnp.concatenate([rows[m - own[0]] if m in own else jnp.zeros((8, R), F32) for m in range(16)], axis=0)
        update = jnp.dot(jnp.concatenate(A, axis=0), padded, precision=HIGH, preferred_element_type=F32)
        for m in range(16):
            if m not in own and m not in ahead:
                new[m] = jnp.where(inside, 0.0, A[m]) - update[8 * m : 8 * m + 8]
        new[own[0]], new[own[1]] = rows
        A = new
    return A


def kernel(
    base, opb, opc, db, dc, fb, fc, fa_out, gn_out,
    bv, cv, st_f, rv_f, rv_d, part_g, y_g, z_g, ag_g, part_m, y_m, z_m, ag_m, inv,
    near, far, base_v, in_sem, op_sem, f_s, f_r, d_s, d_r, yg_s, yg_r, zg_s, zg_r, ag_s, ag_r, ym_s, ym_r, zm_s, zm_r, am_s, am_r,
):
    r, c = lax.axis_index("row"), lax.axis_index("col")
    x, core = r // 2, lax.rem(r, 2)
    z, y = c // NY, lax.rem(c, NY)

    def at_row(dx, dcore):
        return lax.rem(x + dx, NX) * 2 + lax.rem(core + dcore, NC)

    def at_col(dz, dy):
        return lax.rem(z + dz, NZ) * NY + lax.rem(y + dy, NY)

    def remote(src, dst, ss, rs, k, row, col):
        return pltpu.make_async_remote_copy(
            src_ref=src, dst_ref=dst, send_sem=ss.at[k], recv_sem=rs.at[k],
            device_id=(row, col), device_id_type=MESH)

    loads = []
    for g in range(GROUPS):
        rows = pl.ds(8 * g, 8)
        loads.append((pltpu.make_async_copy(opb.at[rows], bv.at[rows], op_sem.at[0, g]),
                      pltpu.make_async_copy(opc.at[rows], cv.at[rows], op_sem.at[1, g])))

    small = [pltpu.make_async_copy(src, dst, in_sem.at[k]) for k, (src, dst) in enumerate((
        (fb, st_f.at[0]), (fc, st_f.at[1]), (db, rv_d.at[r, :, pl.ds(0, 256)]),
        (dc, rv_d.at[r, :, pl.ds(256, 256)]), (base, base_v)))]
    for copy in small:
        copy.start()
    barrier = pltpu.get_barrier_semaphore()
    for dx, dcore, dy, dz in GREETED:
        pl.semaphore_signal(barrier, inc=1, device_id=(at_row(dx, dcore), at_col(dz, dy)), device_id_type=MESH)
    for pair in loads:
        for copy in pair:
            copy.start()
    for copy in small:
        copy.wait()
    rv_f[r] = st_f[core]
    pl.semaphore_wait(barrier, len(GREETED))

    def tell(sem, dz):
        for d in (dz, NZ - dz):
            pl.semaphore_signal(sem, inc=1, device_id=(r, at_col(d, 0)), device_id_type=MESH)

    sent = []
    send_f, send_d = [], []
    for k, (dx, dcore) in enumerate(ROW_OFFS):
        send_f.append(remote(st_f.at[lax.rem(core + dcore, NC)], rv_f.at[r], f_s, f_r, k, at_row(dx, dcore), c))
        send_f[-1].start()
    for k, (dx, dcore) in enumerate(ROW_OFFS):
        send_d.append(remote(rv_d.at[r], rv_d.at[r], d_s, d_r, k, at_row(dx, dcore), c))
        send_d[-1].start()
    sent += send_f + send_d

    tell(near, 1)

    for copy in send_f:
        copy.wait_recv()
    mine = rv_f[pl.ds(2 * x, 2)].reshape(32, 256)
    gram = lax.dot_general(mine, rv_f[...].reshape(R, 256), (((1,), (1,)), ((), ())),
                           precision=HIGH, preferred_element_type=F32)
    part_g[...] = gram.reshape(NY, 8, R)
    send_yg = []
    for dy in range(1, NY):
        send_yg.append(remote(part_g.at[lax.rem(y + dy, NY)], y_g.at[dy - 1], yg_s, yg_r, dy - 1, r, at_col(0, dy)))
        send_yg[-1].start()

    pl.semaphore_wait(near, 2)
    tell(far, 2)
    for copy in send_d:
        copy.wait_recv()
    lanes = lax.rem(lax.broadcasted_iota(jnp.int32, (R, 2 * R), 1), R)
    eye = lax.broadcasted_iota(jnp.int32, (R, 2 * R), 0) == lanes
    for g in range(GROUPS):
        for copy in loads[g]:
            copy.wait()
        d_b = rv_d[:, :, 0:256].reshape(R, 256)
        d_c = rv_d[:, :, 256:512].reshape(R, 256)
        found = []
        for i in range(8 * g, 8 * g + 8, 2):
            both = jnp.dot(d_b, jnp.concatenate([bv[i], bv[i + 1]], axis=1), preferred_element_type=F32)
            both = both + jnp.dot(d_c, jnp.concatenate([cv[i], cv[i + 1]], axis=1), preferred_element_type=F32)
            pair = jnp.sum(jnp.where(eye, both, 0.0), axis=0, keepdims=True)
            found += [pair[:, :R], pair[:, R:]]
        part_m[g // 2, pl.ds(8 * (g % 2), 8), :] = jnp.concatenate(found, axis=0)
    send_ym = []
    for dy in range(1, NY):
        send_ym.append(remote(part_m.at[lax.rem(y + dy, NY)], y_m.at[dy - 1], ym_s, ym_r, dy - 1, r, at_col(0, dy)))
        send_ym[-1].start()

    for copy in send_yg:
        copy.wait_recv()
    z_g[z] = (part_g[y] + y_g[0]) + (y_g[1] + y_g[2])
    pl.semaphore_wait(far, 2)
    send_zg = []
    for dz in range(1, NZ):
        send_zg.append(remote(z_g.at[z], z_g.at[z], zg_s, zg_r, dz - 1, r, at_col(dz, 0)))
        send_zg[-1].start()

    for copy in send_ym:
        copy.wait_recv()
    z_m[z] = (part_m[y] + y_m[0]) + (y_m[1] + y_m[2])
    send_zm = []
    for dz in range(1, NZ):
        send_zm.append(remote(z_m.at[z], z_m.at[z], zm_s, zm_r, dz - 1, r, at_col(dz, 0)))
        send_zm[-1].start()

    for copy in send_zg:
        copy.wait_recv()
    ag_g[r, y] = ((z_g[0] + z_g[1]) + (z_g[2] + z_g[3])) + ((z_g[4] + z_g[5]) + (z_g[6] + z_g[7]))
    send_ag = []
    for k, (dx, dcore, dy) in enumerate(XY_OFFS):
        send_ag.append(remote(ag_g.at[r, y], ag_g.at[r, y], ag_s, ag_r, k, at_row(dx, dcore), at_col(0, dy)))
        send_ag[-1].start()

    for copy in send_zm:
        copy.wait_recv()
    summed = ((z_m[0] + z_m[1]) + (z_m[2] + z_m[3])) + ((z_m[4] + z_m[5]) + (z_m[6] + z_m[7]))
    ag_m[r, y] = base_v[pl.ds(pl.multiple_of(16 * y, 16), 16), :] + summed
    send_am = []
    for k, (dx, dcore, dy) in enumerate(XY_OFFS):
        send_am.append(remote(ag_m.at[r, y], ag_m.at[r, y], am_s, am_r, k, at_row(dx, dcore), at_col(0, dy)))
        send_am[-1].start()

    for copy in send_ag:
        copy.wait_recv()
    gathered = ag_g[...].reshape(NX, NC, 32, R)
    gram_b = gathered[:, 0].reshape(R, R)
    gram_c = gathered[:, 1].reshape(R, R) / K
    hadamard = gram_b / J * gram_c
    blocks = invert([hadamard[8 * m : 8 * m + 8, :] for m in range(16)])
    for m in range(16):
        inv[8 * m : 8 * m + 8, :] = blocks[m]

    for copy in send_am:
        copy.wait_recv()
    whole = ag_m[...].reshape(ROWS, R)
    mtm = lax.dot_general(whole, whole, (((0,), (0,)), ((), ())), precision=HIGH, preferred_element_type=F32)
    inverse = inv[...]
    own = ag_m[r].reshape(64, R)
    fa_out[...] = jnp.dot(own, inverse, precision=HIGH, preferred_element_type=F32)
    half = jnp.dot(mtm, inverse, precision=HIGH, preferred_element_type=F32)
    gram_a = lax.dot_general(inverse, half, (((0,), (0,)), ((), ())), precision=HIGH, preferred_element_type=F32)
    gn_out[...] = gram_a / ROWS * gram_c

    for copy in sent + send_yg + send_zg + send_ag + send_ym + send_zm + send_am:
        copy.wait_send()


def shards(base_mttkrp, operator_b, operator_c, delta_b, delta_c, factor_b, factor_c):
    args = (base_mttkrp, operator_b, operator_c, delta_b.T, delta_c.T, factor_b.T, factor_c.T)
    vmem = pl.BlockSpec(memory_space=pltpu.VMEM)
    hbm = pl.BlockSpec(memory_space=pltpu.HBM)

    def sems(*counts):
        return [pltpu.SemaphoreType.DMA((n,)) for n in counts for _ in range(2)]

    return pl.pallas_call(
        kernel,
        out_shape=(pltpu.VMEM((64, R), F32), pltpu.VMEM((R, R), F32)),
        in_specs=[hbm] * 7,
        out_specs=(vmem, vmem),
        scratch_shapes=[
            pltpu.VMEM((64, 256, R), BF16),
            pltpu.VMEM((64, 256, R), BF16),
            pltpu.VMEM((2, 16, 256), F32),
            pltpu.VMEM((8, 16, 256), F32),
            pltpu.VMEM((8, 16, 512), BF16),
            pltpu.VMEM((NY, 8, R), F32),
            pltpu.VMEM((NY - 1, 8, R), F32),
            pltpu.VMEM((NZ, 8, R), F32),
            pltpu.VMEM((8, NY, 8, R), F32),
            pltpu.VMEM((NY, 16, R), F32),
            pltpu.VMEM((NY - 1, 16, R), F32),
            pltpu.VMEM((NZ, 16, R), F32),
            pltpu.VMEM((8, NY, 16, R), F32),
            pltpu.VMEM((R, R), F32),
            pltpu.SemaphoreType.REGULAR,
            pltpu.SemaphoreType.REGULAR,
            pltpu.VMEM((64, R), F32),
            pltpu.SemaphoreType.DMA((5,)),
            pltpu.SemaphoreType.DMA((2, GROUPS)),
        ] + sems(7, 7, 3, 7, 31, 3, 7, 31),
        compiler_params=pltpu.CompilerParams(
            collective_id=0, has_side_effects=True, vmem_limit_bytes=40 * 2**20),
        name="update",
    )(*(pltpu.with_memory_space_constraint(a, pltpu.HBM) for a in args))


def solution(mesh):
    return jax.shard_map(
        shards,
        mesh=mesh,
        in_specs=(
            P("row", None),
            P("row", "col", None),
            P("row", "col", None),
            P("col", "row"),
            P("col", "row"),
            P("col", "row"),
            P("col", "row"),
        ),
        out_specs=(P("row", None), P()),
        check_vma=False,
    )
```

```python
import functools

import jax
import jax.numpy as jnp
from jax import lax
from jax.experimental import pallas as pl
from jax.experimental.pallas import tpu as pltpu
from jax.sharding import PartitionSpec as P

J = 8192
K = 8192
ROWS = 512
R = 128
F32 = jnp.float32
BF16 = jnp.bfloat16
HIGH = lax.Precision.HIGHEST
MESH = pl.DeviceIdType.MESH

NX, NC, NY, NZ = 4, 2, 4, 8
ROW_OFFS = [(2, 1), (1, 1), (3, 1), (2, 0), (1, 0), (3, 0), (0, 1)]
XY_OFFS = [(dx, dc, dy) for dy in range(NY) for dx in range(NX) for dc in range(NC) if dx or dc or dy]
GREETED = [(dx, dc, 0, 0) for dx, dc in ROW_OFFS[:4]] + [(0, 0, 2, 0)] + [(dx, dc, 0, 0) for dx, dc in ROW_OFFS[4:]] + [(0, 0, 1, 0), (0, 0, 3, 0), (0, 0, 0, 1), (0, 0, 0, 7)]
SAME_CORE = sorted([(dx, dy) for dx in range(NX) for dy in range(NY) if dx or dy], key=lambda o: -(min(o[0], 4 - o[0]) + min(o[1], 4 - o[1])))
HOOK = 6
CHUNKS = 2
GROUPS = 8


def lane_bcast(v, lane):
    return jnp.broadcast_to(v[:, lane : lane + 1], (8, R))


def sub_bcast(v, sub):
    return jnp.broadcast_to(v[sub : sub + 1, :], (8, R))


def invert(A, between):
    lane = lax.broadcasted_iota(jnp.int32, (8, R), 1)
    sub = lax.broadcasted_iota(jnp.int32, (8, R), 0)
    A = list(A)
    for p in range(R // 16):
        between(p)
        l0 = 16 * p
        inside = (lane >= l0) & (lane < l0 + 16)
        own = [2 * p, 2 * p + 1]
        ahead = [m for m in (2 * p + 2, 2 * p + 3) if m < 16]
        c = [[lane_bcast(A[u], l0 + i) for u in own] for i in range(16)]
        early = {m: [lane_bcast(A[m], l0 + i) for i in range(16)] for m in ahead}
        rows = [jnp.where(inside, jnp.where(lane - l0 == sub + 8 * k, 1.0, 0.0), A[u]) for k, u in enumerate(own)]
        for i in range(0, 16, 2):
            v, s = i // 8, i % 8
            a, b = sub_bcast(c[i][v], s), sub_bcast(c[i + 1][v], s)
            d, e = sub_bcast(c[i][v], s + 1), sub_bcast(c[i + 1][v], s + 1)
            det = 1.0 / (a * e - b * d)
            g0 = [(c[i][u] * e - c[i + 1][u] * d) * det for u in range(2)]
            g1 = [(c[i + 1][u] * a - c[i][u] * b) * det for u in range(2)]
            g0[v] = jnp.where(sub == s, -(e * det), jnp.where(sub == s + 1, d * det, g0[v]))
            g1[v] = jnp.where(sub == s, b * det, jnp.where(sub == s + 1, -(a * det), g1[v]))
            hit = (sub == s) | (sub == s + 1)

            def step(t):
                r0, r1 = sub_bcast(t[v], s), sub_bcast(t[v], s + 1)
                kept = [jnp.where(hit, 0.0, t[u]) if u == v else t[u] for u in range(2)]
                return [kept[u] - (g0[u] * r0 + g1[u] * r1) for u in range(2)]

            for m in range(i + 2, 16):
                c[m] = step(c[m])
            rows = step(rows)
        new = list(A)
        for m in ahead:
            t = [early[m][i] * sub_bcast(rows[i // 8], i % 8) for i in range(16)]
            while len(t) > 1:
                t = [t[q] + t[q + 1] for q in range(0, len(t), 2)]
            new[m] = jnp.where(inside, 0.0, A[m]) - t[0]
        padded = jnp.concatenate([rows[m - own[0]] if m in own else jnp.zeros((8, R), F32) for m in range(16)], axis=0)
        update = jnp.dot(jnp.concatenate(A, axis=0), padded, precision=HIGH, preferred_element_type=F32)
        for m in range(16):
            if m not in own and m not in ahead:
                new[m] = jnp.where(inside, 0.0, A[m]) - update[8 * m : 8 * m + 8]
        new[own[0]], new[own[1]] = rows
        A = new
    return A


def kernel(
    base, opb, opc, db, dc, fb, fc, fa_out, gn_out,
    bv, cv, st_f, rv_f, rv_d, part_g, y_g, z_g, ag_g, part_m, y_m, z_m, ag_m, mtm_v, inv,
    near, far, base_v, in_sem, op_sem, f_s, f_r, d_s, d_r, yg_s, yg_r, zg_s, zg_r, ag_s, ag_r, ym_s, ym_r, zm_s, zm_r, am_s, am_r, mt_s, mt_r,
):
    r, c = lax.axis_index("row"), lax.axis_index("col")
    x, core = r // 2, lax.rem(r, 2)
    z, y = c // NY, lax.rem(c, NY)

    def at_row(dx, dcore):
        return lax.rem(x + dx, NX) * 2 + lax.rem(core + dcore, NC)

    def at_col(dz, dy):
        return lax.rem(z + dz, NZ) * NY + lax.rem(y + dy, NY)

    def remote(src, dst, ss, rs, k, row, col):
        return pltpu.make_async_remote_copy(
            src_ref=src, dst_ref=dst, send_sem=ss.at[k], recv_sem=rs.at[k],
            device_id=(row, col), device_id_type=MESH)

    loads = []
    for g in range(CHUNKS):
        rows = pl.ds(64 // CHUNKS * g, 64 // CHUNKS)
        loads.append((pltpu.make_async_copy(opb.at[rows], bv.at[rows], op_sem.at[0, g]),
                      pltpu.make_async_copy(opc.at[rows], cv.at[rows], op_sem.at[1, g])))

    small = [pltpu.make_async_copy(src, dst, in_sem.at[k]) for k, (src, dst) in enumerate((
        (fb, st_f.at[0]), (fc, st_f.at[1]), (db, rv_d.at[r, :, pl.ds(0, 256)]),
        (dc, rv_d.at[r, :, pl.ds(256, 256)]), (base, base_v)))]
    barrier = pltpu.get_barrier_semaphore()
    for dx, dcore, dy, dz in GREETED:
        pl.semaphore_signal(barrier, inc=1, device_id=(at_row(dx, dcore), at_col(dz, dy)), device_id_type=MESH)
    for copy in small:
        copy.start()
    for copy in small:
        copy.wait()
    rv_f[r] = st_f[core]
    pl.semaphore_wait(barrier, len(GREETED))

    def tell(sem, dz):
        for d in (dz, NZ - dz):
            pl.semaphore_signal(sem, inc=1, device_id=(r, at_col(d, 0)), device_id_type=MESH)

    sent = []
    send_f, send_d = [], []
    for k, (dx, dcore) in enumerate(ROW_OFFS):
        send_f.append(remote(st_f.at[lax.rem(core + dcore, NC)], rv_f.at[r], f_s, f_r, k, at_row(dx, dcore), c))
        send_f[-1].start()
    for k, (dx, dcore) in enumerate(ROW_OFFS):
        send_d.append(remote(rv_d.at[r], rv_d.at[r], d_s, d_r, k, at_row(dx, dcore), c))
        send_d[-1].start()
    sent += send_f + send_d

    tell(near, 1)
    for pair in loads:
        for copy in pair:
            copy.start()

    for copy in send_f:
        copy.wait_recv()
    mine = rv_f[pl.ds(2 * x, 2)].reshape(32, 256)
    gram = lax.dot_general(mine, rv_f[...].reshape(R, 256), (((1,), (1,)), ((), ())),
                           precision=HIGH, preferred_element_type=F32)
    part_g[...] = gram.reshape(NY, 8, R)
    send_yg = []
    for dy in (2, 1, 3):
        send_yg.append(remote(part_g.at[lax.rem(y + dy, NY)], y_g.at[dy - 1], yg_s, yg_r, dy - 1, r, at_col(0, dy)))
        send_yg[-1].start()

    pl.semaphore_wait(near, 2)
    tell(far, 2)
    for copy in send_d:
        copy.wait_recv()
    lanes = lax.rem(lax.broadcasted_iota(jnp.int32, (R, 2 * R), 1), R)
    eye = lax.broadcasted_iota(jnp.int32, (R, 2 * R), 0) == lanes
    for g in range(GROUPS):
        if g % (GROUPS // CHUNKS) == 0:
            for copy in loads[g // (GROUPS // CHUNKS)]:
                copy.wait()
        d_b = rv_d[:, :, 0:256].reshape(R, 256)
        d_c = rv_d[:, :, 256:512].reshape(R, 256)
        found = []
        for i in range(8 * g, 8 * g + 8, 2):
            both = jnp.dot(d_b, jnp.concatenate([bv[i], bv[i + 1]], axis=1), preferred_element_type=F32)
            both = both + jnp.dot(d_c, jnp.concatenate([cv[i], cv[i + 1]], axis=1), preferred_element_type=F32)
            pair = jnp.sum(jnp.where(eye, both, 0.0), axis=0, keepdims=True)
            found += [pair[:, :R], pair[:, R:]]
        part_m[g // 2, pl.ds(8 * (g % 2), 8), :] = jnp.concatenate(found, axis=0)
    send_ym = []
    for dy in (2, 1, 3):
        send_ym.append(remote(part_m.at[lax.rem(y + dy, NY)], y_m.at[dy - 1], ym_s, ym_r, dy - 1, r, at_col(0, dy)))
        send_ym[-1].start()

    for copy in send_yg:
        copy.wait_recv()
    z_g[z] = (part_g[y] + y_g[0]) + (y_g[1] + y_g[2])
    pl.semaphore_wait(far, 2)
    send_zg = []
    for dz in (4, 3, 5, 2, 6, 1, 7):
        send_zg.append(remote(z_g.at[z], z_g.at[z], zg_s, zg_r, dz - 1, r, at_col(dz, 0)))
        send_zg[-1].start()

    for copy in send_ym:
        copy.wait_recv()
    z_m[z] = (part_m[y] + y_m[0]) + (y_m[1] + y_m[2])
    send_zm = []
    for dz in (4, 3, 5, 2, 6, 1, 7):
        send_zm.append(remote(z_m.at[z], z_m.at[z], zm_s, zm_r, dz - 1, r, at_col(dz, 0)))
        send_zm[-1].start()

    for copy in send_zg:
        copy.wait_recv()
    ag_g[x, core, y] = ((z_g[0] + z_g[1]) + (z_g[2] + z_g[3])) + ((z_g[4] + z_g[5]) + (z_g[6] + z_g[7]))
    send_ag = []
    for k, (dx, dy) in enumerate(SAME_CORE):
        send_ag.append(remote(ag_g.at[x, core, y], ag_g.at[x, core, y], ag_s, ag_r, k, at_row(dx, 0), at_col(0, dy)))
        send_ag[-1].start()

    for copy in send_zm:
        copy.wait_recv()
    summed = ((z_m[0] + z_m[1]) + (z_m[2] + z_m[3])) + ((z_m[4] + z_m[5]) + (z_m[6] + z_m[7]))
    ag_m[x, y] = base_v[pl.ds(pl.multiple_of(16 * y, 16), 16), :] + summed
    send_am = []
    for k, (dx, dy) in enumerate(SAME_CORE):
        send_am.append(remote(ag_m.at[x, y], ag_m.at[x, y], am_s, am_r, k, at_row(dx, 0), at_col(0, dy)))
        send_am[-1].start()

    for copy in sent + send_yg + send_zg + send_ym:
        copy.wait_send()
    for copy in send_ag:
        copy.wait_recv()
    over_g = remote(ag_g.at[:, core], ag_g.at[:, core], ag_s, ag_r, 15, at_row(0, 1), c)
    over_g.start()
    over_g.wait_recv()
    for copy in send_ag + send_zm:
        copy.wait_send()
    gathered = ag_g[...].reshape(NX, NC, 32, R)
    gram_b = gathered[:, 0].reshape(R, R)
    gram_c = gathered[:, 1].reshape(R, R) / K
    hadamard = gram_b / J * gram_c
    whole_sum = []

    def between(panel):
        if panel != HOOK:
            return
        for copy in send_am:
            copy.wait_recv()
        whole = ag_m[...].reshape(ROWS // 2, R)
        mtm_v[core] = lax.dot_general(whole, whole, (((0,), (0,)), ((), ())), precision=HIGH, preferred_element_type=F32)
        whole_sum.append(remote(mtm_v.at[core], mtm_v.at[core], mt_s, mt_r, 0, at_row(0, 1), c))
        whole_sum[0].start()

    blocks = invert([hadamard[8 * m : 8 * m + 8, :] for m in range(16)], between)
    for m in range(16):
        inv[8 * m : 8 * m + 8, :] = blocks[m]
    swap, = whole_sum
    swap.wait_recv()
    mtm = mtm_v[0] + mtm_v[1]
    inverse = inv[...]
    own = ag_m[x].reshape(64, R)
    fa_out[...] = jnp.dot(own, inverse, precision=HIGH, preferred_element_type=F32)
    half = jnp.dot(mtm, inverse, precision=HIGH, preferred_element_type=F32)
    gram_a = lax.dot_general(inverse, half, (((0,), (0,)), ((), ())), precision=HIGH, preferred_element_type=F32)
    gn_out[...] = gram_a / ROWS * gram_c

    for copy in send_am + [swap, over_g]:
        copy.wait_send()


def shards(base_mttkrp, operator_b, operator_c, delta_b, delta_c, factor_b, factor_c):
    args = (base_mttkrp, operator_b, operator_c, delta_b.T, delta_c.T, factor_b.T, factor_c.T)
    vmem = pl.BlockSpec(memory_space=pltpu.VMEM)
    hbm = pl.BlockSpec(memory_space=pltpu.HBM)

    def sems(*counts):
        return [pltpu.SemaphoreType.DMA((n,)) for n in counts for _ in range(2)]

    return pl.pallas_call(
        kernel,
        out_shape=(pltpu.VMEM((64, R), F32), pltpu.VMEM((R, R), F32)),
        in_specs=[hbm] * 7,
        out_specs=(vmem, vmem),
        scratch_shapes=[
            pltpu.VMEM((64, 256, R), BF16),
            pltpu.VMEM((64, 256, R), BF16),
            pltpu.VMEM((2, 16, 256), F32),
            pltpu.VMEM((8, 16, 256), F32),
            pltpu.VMEM((8, 16, 512), BF16),
            pltpu.VMEM((NY, 8, R), F32),
            pltpu.VMEM((NY - 1, 8, R), F32),
            pltpu.VMEM((NZ, 8, R), F32),
            pltpu.VMEM((NX, NC, NY, 8, R), F32),
            pltpu.VMEM((NY, 16, R), F32),
            pltpu.VMEM((NY - 1, 16, R), F32),
            pltpu.VMEM((NZ, 16, R), F32),
            pltpu.VMEM((NX, NY, 16, R), F32),
            pltpu.VMEM((NC, R, R), F32),
            pltpu.VMEM((R, R), F32),
            pltpu.SemaphoreType.REGULAR,
            pltpu.SemaphoreType.REGULAR,
            pltpu.VMEM((64, R), F32),
            pltpu.SemaphoreType.DMA((5,)),
            pltpu.SemaphoreType.DMA((2, CHUNKS)),
        ] + sems(7, 7, 3, 7, 16, 3, 7, 15, 1),
        compiler_params=pltpu.CompilerParams(
            collective_id=0, has_side_effects=True, vmem_limit_bytes=40 * 2**20),
        name="update",
    )(*(pltpu.with_memory_space_constraint(a, pltpu.HBM) for a in args))


def solution(mesh):
    return jax.shard_map(
        shards,
        mesh=mesh,
        in_specs=(
            P("row", None),
            P("row", "col", None),
            P("row", "col", None),
            P("col", "row"),
            P("col", "row"),
            P("col", "row"),
            P("col", "row"),
        ),
        out_specs=(P("row", None), P()),
        check_vma=False,
    )
```

```python
import functools

import jax
import jax.numpy as jnp
from jax import lax
from jax.experimental import pallas as pl
from jax.experimental.pallas import tpu as pltpu
from jax.sharding import PartitionSpec as P

J = 8192
K = 8192
ROWS = 512
R = 128
F32 = jnp.float32
BF16 = jnp.bfloat16
HIGH = lax.Precision.HIGHEST
MESH = pl.DeviceIdType.MESH

NX, NC, NY, NZ = 4, 2, 4, 8
XY_OFFS = [(dx, dc, dy) for dy in range(NY) for dx in range(NX) for dc in range(NC) if dx or dc or dy]
GREETED = [(2, 0, 0, 0), (0, 0, 2, 0), (1, 0, 0, 0), (3, 0, 0, 0), (0, 0, 1, 0), (0, 0, 3, 0), (0, 0, 0, 1), (0, 0, 0, 7), (0, 1, 0, 0)]
SAME_CORE = sorted([(dx, dy) for dx in range(NX) for dy in range(NY) if dx or dy], key=lambda o: -(min(o[0], 4 - o[0]) + min(o[1], 4 - o[1])))
HOOK = 6
CHUNKS = 2
GROUPS = 8


def lane_bcast(v, lane):
    return jnp.broadcast_to(v[:, lane : lane + 1], (8, R))


def sub_bcast(v, sub):
    return jnp.broadcast_to(v[sub : sub + 1, :], (8, R))


def invert(A, between):
    lane = lax.broadcasted_iota(jnp.int32, (8, R), 1)
    sub = lax.broadcasted_iota(jnp.int32, (8, R), 0)
    A = list(A)
    for p in range(R // 16):
        between(p)
        l0 = 16 * p
        inside = (lane >= l0) & (lane < l0 + 16)
        own = [2 * p, 2 * p + 1]
        ahead = [m for m in (2 * p + 2, 2 * p + 3) if m < 16]
        c = [[lane_bcast(A[u], l0 + i) for u in own] for i in range(16)]
        early = {m: [lane_bcast(A[m], l0 + i) for i in range(16)] for m in ahead}
        rows = [jnp.where(inside, jnp.where(lane - l0 == sub + 8 * k, 1.0, 0.0), A[u]) for k, u in enumerate(own)]
        for i in range(0, 16, 2):
            v, s = i // 8, i % 8
            a, b = sub_bcast(c[i][v], s), sub_bcast(c[i + 1][v], s)
            d, e = sub_bcast(c[i][v], s + 1), sub_bcast(c[i + 1][v], s + 1)
            det = 1.0 / (a * e - b * d)
            g0 = [(c[i][u] * e - c[i + 1][u] * d) * det for u in range(2)]
            g1 = [(c[i + 1][u] * a - c[i][u] * b) * det for u in range(2)]
            g0[v] = jnp.where(sub == s, -(e * det), jnp.where(sub == s + 1, d * det, g0[v]))
            g1[v] = jnp.where(sub == s, b * det, jnp.where(sub == s + 1, -(a * det), g1[v]))
            hit = (sub == s) | (sub == s + 1)

            def step(t):
                r0, r1 = sub_bcast(t[v], s), sub_bcast(t[v], s + 1)
                kept = [jnp.where(hit, 0.0, t[u]) if u == v else t[u] for u in range(2)]
                return [kept[u] - (g0[u] * r0 + g1[u] * r1) for u in range(2)]

            for m in range(i + 2, 16):
                c[m] = step(c[m])
            rows = step(rows)
        new = list(A)
        for m in ahead:
            t = [early[m][i] * sub_bcast(rows[i // 8], i % 8) for i in range(16)]
            while len(t) > 1:
                t = [t[q] + t[q + 1] for q in range(0, len(t), 2)]
            new[m] = jnp.where(inside, 0.0, A[m]) - t[0]
        padded = jnp.concatenate([rows[m - own[0]] if m in own else jnp.zeros((8, R), F32) for m in range(16)], axis=0)
        update = jnp.dot(jnp.concatenate(A, axis=0), padded, precision=HIGH, preferred_element_type=F32)
        for m in range(16):
            if m not in own and m not in ahead:
                new[m] = jnp.where(inside, 0.0, A[m]) - update[8 * m : 8 * m + 8]
        new[own[0]], new[own[1]] = rows
        A = new
    return A


def kernel(
    base, opb, opc, db, dc, fb, fc, fa_out, gn_out,
    bv, cv, st_f, pass_f, rv_f, rv_d, part_g, y_g, z_g, ag_g, part_m, y_m, z_m, ag_m, mtm_v, inv,
    near, far, base_v, in_sem, op_sem, p_s, p_r, f_s, f_r, d_s, d_r, yg_s, yg_r, zg_s, zg_r, ag_s, ag_r, ym_s, ym_r, zm_s, zm_r, am_s, am_r, mt_s, mt_r,
):
    r, c = lax.axis_index("row"), lax.axis_index("col")
    x, core = r // 2, lax.rem(r, 2)
    z, y = c // NY, lax.rem(c, NY)

    def at_row(dx, dcore):
        return lax.rem(x + dx, NX) * 2 + lax.rem(core + dcore, NC)

    def at_col(dz, dy):
        return lax.rem(z + dz, NZ) * NY + lax.rem(y + dy, NY)

    def remote(src, dst, ss, rs, k, row, col):
        return pltpu.make_async_remote_copy(
            src_ref=src, dst_ref=dst, send_sem=ss.at[k], recv_sem=rs.at[k],
            device_id=(row, col), device_id_type=MESH)

    loads = []
    for g in range(CHUNKS):
        rows = pl.ds(64 // CHUNKS * g, 64 // CHUNKS)
        loads.append((pltpu.make_async_copy(opb.at[rows], bv.at[rows], op_sem.at[0, g]),
                      pltpu.make_async_copy(opc.at[rows], cv.at[rows], op_sem.at[1, g])))

    small = [pltpu.make_async_copy(src, dst, in_sem.at[k]) for k, (src, dst) in enumerate((
        (fb, st_f.at[0]), (fc, st_f.at[1]), (db, rv_d.at[x, core, :, pl.ds(0, 256)]),
        (dc, rv_d.at[x, core, :, pl.ds(256, 256)]), (base, base_v)))]
    barrier = pltpu.get_barrier_semaphore()
    for dx, dcore, dy, dz in GREETED:
        pl.semaphore_signal(barrier, inc=1, device_id=(at_row(dx, dcore), at_col(dz, dy)), device_id_type=MESH)
    for copy in small:
        copy.start()
    for copy in small:
        copy.wait()
    rv_f[x, core] = st_f[core]
    pass_f[x] = st_f[1 - core]
    pl.semaphore_wait(barrier, len(GREETED))

    def tell(sem, dz):
        for d in (dz, NZ - dz):
            pl.semaphore_signal(sem, inc=1, device_id=(r, at_col(d, 0)), device_id_type=MESH)

    sent = []
    pass_in, send_f, send_d = [], [], []
    for k, dx in enumerate((2, 1, 3)):
        pass_in.append(remote(st_f.at[1 - core], pass_f.at[x], p_s, p_r, k, at_row(dx, 0), c))
        pass_in[-1].start()
    for k, dx in enumerate((2, 1, 3)):
        send_d.append(remote(rv_d.at[x, core], rv_d.at[x, core], d_s, d_r, k, at_row(dx, 0), c))
        send_d[-1].start()
    for k, dx in enumerate((2, 1, 3)):
        send_f.append(remote(st_f.at[core], rv_f.at[x, core], f_s, f_r, k, at_row(dx, 0), c))
        send_f[-1].start()
    tell(near, 1)
    for pair in loads:
        for copy in pair:
            copy.start()

    for copy in pass_in:
        copy.wait_recv()
    over_f = remote(pass_f, rv_f.at[:, core], f_s, f_r, 3, at_row(0, 1), c)
    over_f.start()

    for copy in send_d:
        copy.wait_recv()
    over_d = remote(rv_d.at[:, core], rv_d.at[:, core], d_s, d_r, 3, at_row(0, 1), c)
    over_d.start()
    for copy in send_f + [over_f]:
        copy.wait_recv()
    mine = rv_f[x].reshape(32, 256)
    gram = lax.dot_general(mine, rv_f[...].reshape(R, 256), (((1,), (1,)), ((), ())),
                           precision=HIGH, preferred_element_type=F32)
    part_g[...] = gram.reshape(NY, 8, R)
    send_yg = []
    for dy in (2, 1, 3):
        send_yg.append(remote(part_g.at[lax.rem(y + dy, NY)], y_g.at[dy - 1], yg_s, yg_r, dy - 1, r, at_col(0, dy)))
        send_yg[-1].start()

    pl.semaphore_wait(near, 2)
    tell(far, 2)
    over_d.wait_recv()
    sent += pass_in + send_f + send_d + [over_f, over_d]
    lanes = lax.rem(lax.broadcasted_iota(jnp.int32, (R, 2 * R), 1), R)
    eye = lax.broadcasted_iota(jnp.int32, (R, 2 * R), 0) == lanes
    for g in range(GROUPS):
        if g % (GROUPS // CHUNKS) == 0:
            for copy in loads[g // (GROUPS // CHUNKS)]:
                copy.wait()
        d_b = rv_d[:, :, :, 0:256].reshape(R, 256)
        d_c = rv_d[:, :, :, 256:512].reshape(R, 256)
        found = []
        for i in range(8 * g, 8 * g + 8, 2):
            both = jnp.dot(d_b, jnp.concatenate([bv[i], bv[i + 1]], axis=1), preferred_element_type=F32)
            both = both + jnp.dot(d_c, jnp.concatenate([cv[i], cv[i + 1]], axis=1), preferred_element_type=F32)
            pair = jnp.sum(jnp.where(eye, both, 0.0), axis=0, keepdims=True)
            found += [pair[:, :R], pair[:, R:]]
        part_m[g // 2, pl.ds(8 * (g % 2), 8), :] = jnp.concatenate(found, axis=0)
    send_ym = []
    for dy in (2, 1, 3):
        send_ym.append(remote(part_m.at[lax.rem(y + dy, NY)], y_m.at[dy - 1], ym_s, ym_r, dy - 1, r, at_col(0, dy)))
        send_ym[-1].start()

    for copy in send_yg:
        copy.wait_recv()
    z_g[z] = (part_g[y] + y_g[0]) + (y_g[1] + y_g[2])
    pl.semaphore_wait(far, 2)
    send_zg = []
    for dz in (4, 3, 5, 2, 6, 1, 7):
        send_zg.append(remote(z_g.at[z], z_g.at[z], zg_s, zg_r, dz - 1, r, at_col(dz, 0)))
        send_zg[-1].start()

    for copy in send_ym:
        copy.wait_recv()
    z_m[z] = (part_m[y] + y_m[0]) + (y_m[1] + y_m[2])
    send_zm = []
    for dz in (4, 3, 5, 2, 6, 1, 7):
        send_zm.append(remote(z_m.at[z], z_m.at[z], zm_s, zm_r, dz - 1, r, at_col(dz, 0)))
        send_zm[-1].start()

    for copy in send_zg:
        copy.wait_recv()
    ag_g[x, core, y] = ((z_g[0] + z_g[1]) + (z_g[2] + z_g[3])) + ((z_g[4] + z_g[5]) + (z_g[6] + z_g[7]))
    send_ag = []
    for k, (dx, dy) in enumerate(SAME_CORE):
        send_ag.append(remote(ag_g.at[x, core, y], ag_g.at[x, core, y], ag_s, ag_r, k, at_row(dx, 0), at_col(0, dy)))
        send_ag[-1].start()

    for copy in send_zm:
        copy.wait_recv()
    summed = ((z_m[0] + z_m[1]) + (z_m[2] + z_m[3])) + ((z_m[4] + z_m[5]) + (z_m[6] + z_m[7]))
    ag_m[x, y] = base_v[pl.ds(pl.multiple_of(16 * y, 16), 16), :] + summed
    send_am = []
    for k, (dx, dy) in enumerate(SAME_CORE):
        send_am.append(remote(ag_m.at[x, y], ag_m.at[x, y], am_s, am_r, k, at_row(dx, 0), at_col(0, dy)))
        send_am[-1].start()

    for copy in sent + send_yg + send_zg + send_ym:
        copy.wait_send()
    for copy in send_ag:
        copy.wait_recv()
    over_g = remote(ag_g.at[:, core], ag_g.at[:, core], ag_s, ag_r, 15, at_row(0, 1), c)
    over_g.start()
    over_g.wait_recv()
    for copy in send_ag + send_zm:
        copy.wait_send()
    gathered = ag_g[...].reshape(NX, NC, 32, R)
    gram_b = gathered[:, 0].reshape(R, R)
    gram_c = gathered[:, 1].reshape(R, R) / K
    hadamard = gram_b / J * gram_c
    whole_sum = []

    def between(panel):
        if panel != HOOK:
            return
        for copy in send_am:
            copy.wait_recv()
        whole = ag_m[...].reshape(ROWS // 2, R)
        mtm_v[core] = lax.dot_general(whole, whole, (((0,), (0,)), ((), ())), precision=HIGH, preferred_element_type=F32)
        whole_sum.append(remote(mtm_v.at[core], mtm_v.at[core], mt_s, mt_r, 0, at_row(0, 1), c))
        whole_sum[0].start()

    blocks = invert([hadamard[8 * m : 8 * m + 8, :] for m in range(16)], between)
    for m in range(16):
        inv[8 * m : 8 * m + 8, :] = blocks[m]
    swap, = whole_sum
    swap.wait_recv()
    mtm = mtm_v[0] + mtm_v[1]
    inverse = inv[...]
    own = ag_m[x].reshape(64, R)
    fa_out[...] = jnp.dot(own, inverse, precision=HIGH, preferred_element_type=F32)
    half = jnp.dot(mtm, inverse, precision=HIGH, preferred_element_type=F32)
    gram_a = lax.dot_general(inverse, half, (((0,), (0,)), ((), ())), precision=HIGH, preferred_element_type=F32)
    gn_out[...] = gram_a / ROWS * gram_c

    for copy in send_am + [swap, over_g]:
        copy.wait_send()


def deliver(fa, gn, fa_out, gn_out, sem):
    copies = [pltpu.make_async_copy(src, dst, sem.at[k]) for k, (src, dst) in enumerate(((fa, fa_out), (gn, gn_out)))]
    for copy in copies:
        copy.start()
    for copy in copies:
        copy.wait()


def shards(base_mttkrp, operator_b, operator_c, delta_b, delta_c, factor_b, factor_c):
    args = (base_mttkrp, operator_b, operator_c, delta_b.T, delta_c.T, factor_b.T, factor_c.T)
    vmem = pl.BlockSpec(memory_space=pltpu.VMEM)
    hbm = pl.BlockSpec(memory_space=pltpu.HBM)

    def sems(*counts):
        return [pltpu.SemaphoreType.DMA((n,)) for n in counts for _ in range(2)]

    solved = pl.pallas_call(
        kernel,
        out_shape=(pltpu.VMEM((64, R), F32), pltpu.VMEM((R, R), F32)),
        in_specs=[hbm] * 7,
        out_specs=(vmem, vmem),
        scratch_shapes=[
            pltpu.VMEM((64, 256, R), BF16),
            pltpu.VMEM((64, 256, R), BF16),
            pltpu.VMEM((2, 16, 256), F32),
            pltpu.VMEM((NX, 16, 256), F32),
            pltpu.VMEM((NX, NC, 16, 256), F32),
            pltpu.VMEM((NX, NC, 16, 512), BF16),
            pltpu.VMEM((NY, 8, R), F32),
            pltpu.VMEM((NY - 1, 8, R), F32),
            pltpu.VMEM((NZ, 8, R), F32),
            pltpu.VMEM((NX, NC, NY, 8, R), F32),
            pltpu.VMEM((NY, 16, R), F32),
            pltpu.VMEM((NY - 1, 16, R), F32),
            pltpu.VMEM((NZ, 16, R), F32),
            pltpu.VMEM((NX, NY, 16, R), F32),
            pltpu.VMEM((NC, R, R), F32),
            pltpu.VMEM((R, R), F32),
            pltpu.SemaphoreType.REGULAR,
            pltpu.SemaphoreType.REGULAR,
            pltpu.VMEM((64, R), F32),
            pltpu.SemaphoreType.DMA((5,)),
            pltpu.SemaphoreType.DMA((2, CHUNKS)),
        ] + sems(3, 4, 4, 3, 7, 16, 3, 7, 15, 1),
        compiler_params=pltpu.CompilerParams(
            collective_id=0, has_side_effects=True, vmem_limit_bytes=40 * 2**20),
        name="update",
    )(*(pltpu.with_memory_space_constraint(a, pltpu.HBM) for a in args))
    return pl.pallas_call(
        deliver,
        out_shape=(jax.ShapeDtypeStruct((64, R), F32), jax.ShapeDtypeStruct((R, R), F32)),
        in_specs=[vmem] * 2,
        out_specs=(hbm, hbm),
        scratch_shapes=[pltpu.SemaphoreType.DMA((2,))],
        name="deliver",
    )(*(pltpu.with_memory_space_constraint(a, pltpu.VMEM) for a in solved))


def solution(mesh):
    return jax.shard_map(
        shards,
        mesh=mesh,
        in_specs=(
            P("row", None),
            P("row", "col", None),
            P("row", "col", None),
            P("col", "row"),
            P("col", "row"),
            P("col", "row"),
            P("col", "row"),
        ),
        out_specs=(P("row", None), P()),
        check_vma=False,
    )
```

```python
import functools

import jax
import jax.numpy as jnp
from jax import lax
from jax.experimental import pallas as pl
from jax.experimental.pallas import tpu as pltpu
from jax.sharding import PartitionSpec as P

J = 8192
K = 8192
ROWS = 512
R = 128
F32 = jnp.float32
BF16 = jnp.bfloat16
HIGH = lax.Precision.HIGHEST
MESH = pl.DeviceIdType.MESH

NX, NC, NY, NZ = 4, 2, 4, 8
XY_OFFS = [(dx, dc, dy) for dy in range(NY) for dx in range(NX) for dc in range(NC) if dx or dc or dy]
GREETED = [(2, 0, 0, 0), (0, 0, 2, 0), (1, 0, 0, 0), (3, 0, 0, 0), (0, 0, 1, 0), (0, 0, 3, 0), (0, 0, 0, 1), (0, 0, 0, 7), (0, 1, 0, 0)]
SAME_CORE = sorted([(dx, dy) for dx in range(NX) for dy in range(NY) if dx or dy], key=lambda o: -(min(o[0], 4 - o[0]) + min(o[1], 4 - o[1])))
HOOK = 6
CHUNKS = 2
GROUPS = 8


def lane_bcast(v, lane):
    return jnp.broadcast_to(v[:, lane : lane + 1], (8, R))


def sub_bcast(v, sub):
    return jnp.broadcast_to(v[sub : sub + 1, :], (8, R))


def invert(A, between):
    lane = lax.broadcasted_iota(jnp.int32, (8, R), 1)
    sub = lax.broadcasted_iota(jnp.int32, (8, R), 0)
    t = [jnp.where(lane == sub + 8 * m, A[m], 0.0) for m in range(16)]
    down = [lax.rsqrt(jnp.sum(d, axis=1, keepdims=True)) for d in t]
    while len(t) > 1:
        t = [t[q] + t[q + 1] for q in range(0, len(t), 2)]
    across = lax.rsqrt(jnp.sum(t[0], axis=0, keepdims=True))
    A = [A[m] * across * down[m] for m in range(16)]
    for p in range(R // 16):
        between(p)
        l0 = 16 * p
        inside = (lane >= l0) & (lane < l0 + 16)
        own = [2 * p, 2 * p + 1]
        ahead = [m for m in (2 * p + 2, 2 * p + 3) if m < 16]
        c = [[lane_bcast(A[u], l0 + i) for u in own] for i in range(16)]
        early = {m: [lane_bcast(A[m], l0 + i) for i in range(16)] for m in ahead}
        rows = [jnp.where(inside, jnp.where(lane - l0 == sub + 8 * k, 1.0, 0.0), A[u]) for k, u in enumerate(own)]
        for i in range(0, 16, 2):
            v, s = i // 8, i % 8
            a, b = sub_bcast(c[i][v], s), sub_bcast(c[i + 1][v], s)
            d, e = sub_bcast(c[i][v], s + 1), sub_bcast(c[i + 1][v], s + 1)
            det = 1.0 / (a * e - b * d)
            g0 = [c[i][u] * e - c[i + 1][u] * d for u in range(2)]
            g1 = [c[i + 1][u] * a - c[i][u] * b for u in range(2)]
            g0[v] = jnp.where(sub == s, -e, jnp.where(sub == s + 1, d, g0[v]))
            g1[v] = jnp.where(sub == s, b, jnp.where(sub == s + 1, -a, g1[v]))
            hit = (sub == s) | (sub == s + 1)

            def step(t):
                r0, r1 = sub_bcast(t[v], s), sub_bcast(t[v], s + 1)
                kept = [jnp.where(hit, 0.0, t[u]) if u == v else t[u] for u in range(2)]
                return [kept[u] - (g0[u] * r0 + g1[u] * r1) * det for u in range(2)]

            for m in range(i + 2, 16):
                c[m] = step(c[m])
            rows = step(rows)
        new = list(A)
        for m in ahead:
            t = [early[m][i] * sub_bcast(rows[i // 8], i % 8) for i in range(16)]
            while len(t) > 1:
                t = [t[q] + t[q + 1] for q in range(0, len(t), 2)]
            new[m] = jnp.where(inside, 0.0, A[m]) - t[0]
        padded = jnp.concatenate([rows[m - own[0]] if m in own else jnp.zeros((8, R), F32) for m in range(16)], axis=0)
        update = jnp.dot(jnp.concatenate(A, axis=0), padded, precision=HIGH, preferred_element_type=F32)
        for m in range(16):
            if m not in own and m not in ahead:
                new[m] = jnp.where(inside, 0.0, A[m]) - update[8 * m : 8 * m + 8]
        new[own[0]], new[own[1]] = rows
        A = new
    return [A[m] * across * down[m] for m in range(16)]


def kernel(
    base, opb, opc, db, dc, fb, fc, fa_out, gn_out,
    bv, cv, st_f, pass_f, rv_f, rv_d, part_g, y_g, z_g, ag_g, part_m, y_m, z_m, ag_m, mtm_v, inv,
    near, far, base_v, in_sem, op_sem, p_s, p_r, f_s, f_r, d_s, d_r, yg_s, yg_r, zg_s, zg_r, ag_s, ag_r, ym_s, ym_r, zm_s, zm_r, am_s, am_r, mt_s, mt_r,
):
    r, c = lax.axis_index("row"), lax.axis_index("col")
    x, core = r // 2, lax.rem(r, 2)
    z, y = c // NY, lax.rem(c, NY)

    def at_row(dx, dcore):
        return lax.rem(x + dx, NX) * 2 + lax.rem(core + dcore, NC)

    def at_col(dz, dy):
        return lax.rem(z + dz, NZ) * NY + lax.rem(y + dy, NY)

    def remote(src, dst, ss, rs, k, row, col):
        return pltpu.make_async_remote_copy(
            src_ref=src, dst_ref=dst, send_sem=ss.at[k], recv_sem=rs.at[k],
            device_id=(row, col), device_id_type=MESH)

    loads = []
    for g in range(CHUNKS):
        rows = pl.ds(64 // CHUNKS * g, 64 // CHUNKS)
        loads.append((pltpu.make_async_copy(opb.at[rows], bv.at[rows], op_sem.at[0, g]),
                      pltpu.make_async_copy(opc.at[rows], cv.at[rows], op_sem.at[1, g])))

    small = [pltpu.make_async_copy(src, dst, in_sem.at[k]) for k, (src, dst) in enumerate((
        (fb, st_f.at[0]), (fc, st_f.at[1]), (db, rv_d.at[x, core, :, pl.ds(0, 256)]),
        (dc, rv_d.at[x, core, :, pl.ds(256, 256)]), (base, base_v)))]
    barrier = pltpu.get_barrier_semaphore()
    for dx, dcore, dy, dz in GREETED:
        pl.semaphore_signal(barrier, inc=1, device_id=(at_row(dx, dcore), at_col(dz, dy)), device_id_type=MESH)
    for copy in small:
        copy.start()
    for copy in small:
        copy.wait()
    rv_f[x, core] = st_f[core]
    pass_f[x] = st_f[1 - core]
    pl.semaphore_wait(barrier, len(GREETED))

    def tell(sem, dz):
        for d in (dz, NZ - dz):
            pl.semaphore_signal(sem, inc=1, device_id=(r, at_col(d, 0)), device_id_type=MESH)

    sent = []
    pass_in, send_f, send_d = [], [], []
    for k, dx in enumerate((2, 1, 3)):
        pass_in.append(remote(st_f.at[1 - core], pass_f.at[x], p_s, p_r, k, at_row(dx, 0), c))
        pass_in[-1].start()
    for k, dx in enumerate((2, 1, 3)):
        send_d.append(remote(rv_d.at[x, core], rv_d.at[x, core], d_s, d_r, k, at_row(dx, 0), c))
        send_d[-1].start()
    for k, dx in enumerate((2, 1, 3)):
        send_f.append(remote(st_f.at[core], rv_f.at[x, core], f_s, f_r, k, at_row(dx, 0), c))
        send_f[-1].start()
    tell(near, 1)
    for pair in loads:
        for copy in pair:
            copy.start()

    for copy in pass_in:
        copy.wait_recv()
    over_f = remote(pass_f, rv_f.at[:, core], f_s, f_r, 3, at_row(0, 1), c)
    over_f.start()

    for copy in send_d:
        copy.wait_recv()
    over_d = remote(rv_d.at[:, core], rv_d.at[:, core], d_s, d_r, 3, at_row(0, 1), c)
    over_d.start()
    for copy in send_f + [over_f]:
        copy.wait_recv()
    mine = rv_f[x].reshape(32, 256)
    gram = lax.dot_general(mine, rv_f[...].reshape(R, 256), (((1,), (1,)), ((), ())),
                           precision=HIGH, preferred_element_type=F32)
    part_g[...] = gram.reshape(NY, 8, R)
    send_yg = []
    for dy in (2, 1, 3):
        send_yg.append(remote(part_g.at[lax.rem(y + dy, NY)], y_g.at[dy - 1], yg_s, yg_r, dy - 1, r, at_col(0, dy)))
        send_yg[-1].start()

    pl.semaphore_wait(near, 2)
    tell(far, 2)
    over_d.wait_recv()
    sent += pass_in + send_f + send_d + [over_f, over_d]
    lanes = lax.rem(lax.broadcasted_iota(jnp.int32, (R, 2 * R), 1), R)
    eye = lax.broadcasted_iota(jnp.int32, (R, 2 * R), 0) == lanes
    for g in range(GROUPS):
        if g % (GROUPS // CHUNKS) == 0:
            for copy in loads[g // (GROUPS // CHUNKS)]:
                copy.wait()
        d_b = rv_d[:, :, :, 0:256].reshape(R, 256)
        d_c = rv_d[:, :, :, 256:512].reshape(R, 256)
        found = []
        for i in range(8 * g, 8 * g + 8, 2):
            both = jnp.dot(d_b, jnp.concatenate([bv[i], bv[i + 1]], axis=1), preferred_element_type=F32)
            both = both + jnp.dot(d_c, jnp.concatenate([cv[i], cv[i + 1]], axis=1), preferred_element_type=F32)
            pair = jnp.sum(jnp.where(eye, both, 0.0), axis=0, keepdims=True)
            found += [pair[:, :R], pair[:, R:]]
        part_m[g // 2, pl.ds(8 * (g % 2), 8), :] = jnp.concatenate(found, axis=0)
    send_ym = []
    for dy in (2, 1, 3):
        send_ym.append(remote(part_m.at[lax.rem(y + dy, NY)], y_m.at[dy - 1], ym_s, ym_r, dy - 1, r, at_col(0, dy)))
        send_ym[-1].start()

    for copy in send_yg:
        copy.wait_recv()
    z_g[z] = (part_g[y] + y_g[0]) + (y_g[1] + y_g[2])
    pl.semaphore_wait(far, 2)
    send_zg = []
    for dz in (4, 3, 5, 2, 6, 1, 7):
        send_zg.append(remote(z_g.at[z], z_g.at[z], zg_s, zg_r, dz - 1, r, at_col(dz, 0)))
        send_zg[-1].start()

    for copy in send_ym:
        copy.wait_recv()
    z_m[z] = (part_m[y] + y_m[0]) + (y_m[1] + y_m[2])
    send_zm = []
    for dz in (4, 3, 5, 2, 6, 1, 7):
        send_zm.append(remote(z_m.at[z], z_m.at[z], zm_s, zm_r, dz - 1, r, at_col(dz, 0)))
        send_zm[-1].start()

    for copy in send_zg:
        copy.wait_recv()
    ag_g[x, core, y] = ((z_g[0] + z_g[1]) + (z_g[2] + z_g[3])) + ((z_g[4] + z_g[5]) + (z_g[6] + z_g[7]))
    send_ag = []
    for k, (dx, dy) in enumerate(SAME_CORE):
        send_ag.append(remote(ag_g.at[x, core, y], ag_g.at[x, core, y], ag_s, ag_r, k, at_row(dx, 0), at_col(0, dy)))
        send_ag[-1].start()

    for copy in send_zm:
        copy.wait_recv()
    summed = ((z_m[0] + z_m[1]) + (z_m[2] + z_m[3])) + ((z_m[4] + z_m[5]) + (z_m[6] + z_m[7]))
    ag_m[x, y] = base_v[pl.ds(pl.multiple_of(16 * y, 16), 16), :] + summed
    send_am = []
    for k, (dx, dy) in enumerate(SAME_CORE):
        send_am.append(remote(ag_m.at[x, y], ag_m.at[x, y], am_s, am_r, k, at_row(dx, 0), at_col(0, dy)))
        send_am[-1].start()

    for copy in sent + send_yg + send_zg + send_ym:
        copy.wait_send()
    for copy in send_ag:
        copy.wait_recv()
    over_g = remote(ag_g.at[:, core], ag_g.at[:, core], ag_s, ag_r, 15, at_row(0, 1), c)
    over_g.start()
    over_g.wait_recv()
    for copy in send_ag + send_zm:
        copy.wait_send()
    gathered = ag_g[...].reshape(NX, NC, 32, R)
    gram_b = gathered[:, 0].reshape(R, R)
    gram_c = gathered[:, 1].reshape(R, R) / K
    hadamard = gram_b / J * gram_c
    whole_sum = []

    def between(panel):
        if panel != HOOK:
            return
        for copy in send_am:
            copy.wait_recv()
        whole = ag_m[...].reshape(ROWS // 2, R)
        mtm_v[core] = lax.dot_general(whole, whole, (((0,), (0,)), ((), ())), precision=HIGH, preferred_element_type=F32)
        whole_sum.append(remote(mtm_v.at[core], mtm_v.at[core], mt_s, mt_r, 0, at_row(0, 1), c))
        whole_sum[0].start()

    blocks = invert([hadamard[8 * m : 8 * m + 8, :] for m in range(16)], between)
    for m in range(16):
        inv[8 * m : 8 * m + 8, :] = blocks[m]
    swap, = whole_sum
    swap.wait_recv()
    mtm = mtm_v[0] + mtm_v[1]
    inverse = inv[...]
    own = ag_m[x].reshape(64, R)
    fa_out[...] = jnp.dot(own, inverse, precision=HIGH, preferred_element_type=F32)
    half = jnp.dot(mtm, inverse, precision=HIGH, preferred_element_type=F32)
    gram_a = lax.dot_general(inverse, half, (((0,), (0,)), ((), ())), precision=HIGH, preferred_element_type=F32)
    gn_out[...] = gram_a / ROWS * gram_c

    for copy in send_am + [swap, over_g]:
        copy.wait_send()


def deliver(fa, gn, fa_out, gn_out, sem):
    copies = [pltpu.make_async_copy(src, dst, sem.at[k]) for k, (src, dst) in enumerate(((fa, fa_out), (gn, gn_out)))]
    for copy in copies:
        copy.start()
    for copy in copies:
        copy.wait()


def shards(base_mttkrp, operator_b, operator_c, delta_b, delta_c, factor_b, factor_c):
    args = (base_mttkrp, operator_b, operator_c, delta_b.T, delta_c.T, factor_b.T, factor_c.T)
    vmem = pl.BlockSpec(memory_space=pltpu.VMEM)
    hbm = pl.BlockSpec(memory_space=pltpu.HBM)

    def sems(*counts):
        return [pltpu.SemaphoreType.DMA((n,)) for n in counts for _ in range(2)]

    solved = pl.pallas_call(
        kernel,
        out_shape=(pltpu.VMEM((64, R), F32), pltpu.VMEM((R, R), F32)),
        in_specs=[hbm] * 7,
        out_specs=(vmem, vmem),
        scratch_shapes=[
            pltpu.VMEM((64, 256, R), BF16),
            pltpu.VMEM((64, 256, R), BF16),
            pltpu.VMEM((2, 16, 256), F32),
            pltpu.VMEM((NX, 16, 256), F32),
            pltpu.VMEM((NX, NC, 16, 256), F32),
            pltpu.VMEM((NX, NC, 16, 512), BF16),
            pltpu.VMEM((NY, 8, R), F32),
            pltpu.VMEM((NY - 1, 8, R), F32),
            pltpu.VMEM((NZ, 8, R), F32),
            pltpu.VMEM((NX, NC, NY, 8, R), F32),
            pltpu.VMEM((NY, 16, R), F32),
            pltpu.VMEM((NY - 1, 16, R), F32),
            pltpu.VMEM((NZ, 16, R), F32),
            pltpu.VMEM((NX, NY, 16, R), F32),
            pltpu.VMEM((NC, R, R), F32),
            pltpu.VMEM((R, R), F32),
            pltpu.SemaphoreType.REGULAR,
            pltpu.SemaphoreType.REGULAR,
            pltpu.VMEM((64, R), F32),
            pltpu.SemaphoreType.DMA((5,)),
            pltpu.SemaphoreType.DMA((2, CHUNKS)),
        ] + sems(3, 4, 4, 3, 7, 16, 3, 7, 15, 1),
        compiler_params=pltpu.CompilerParams(
            collective_id=0, has_side_effects=True, vmem_limit_bytes=40 * 2**20),
        name="update",
    )(*(pltpu.with_memory_space_constraint(a, pltpu.HBM) for a in args))
    return pl.pallas_call(
        deliver,
        out_shape=(jax.ShapeDtypeStruct((64, R), F32), jax.ShapeDtypeStruct((R, R), F32)),
        in_specs=[vmem] * 2,
        out_specs=(hbm, hbm),
        scratch_shapes=[pltpu.SemaphoreType.DMA((2,))],
        name="deliver",
    )(*(pltpu.with_memory_space_constraint(a, pltpu.VMEM) for a in solved))


def solution(mesh):
    return jax.shard_map(
        shards,
        mesh=mesh,
        in_specs=(
            P("row", None),
            P("row", "col", None),
            P("row", "col", None),
            P("col", "row"),
            P("col", "row"),
            P("col", "row"),
            P("col", "row"),
        ),
        out_specs=(P("row", None), P()),
        check_vma=False,
    )
```

```python
import functools

import jax
import jax.numpy as jnp
from jax import lax
from jax.experimental import pallas as pl
from jax.experimental.pallas import tpu as pltpu
from jax.sharding import PartitionSpec as P

J = 8192
K = 8192
ROWS = 512
R = 128
F32 = jnp.float32
BF16 = jnp.bfloat16
HIGH = lax.Precision.HIGHEST
MESH = pl.DeviceIdType.MESH

NX, NC, NY, NZ = 4, 2, 4, 8
XY_OFFS = [(dx, dc, dy) for dy in range(NY) for dx in range(NX) for dc in range(NC) if dx or dc or dy]
GREETED = [(2, 0, 0, 0), (0, 0, 2, 0), (1, 0, 0, 0), (3, 0, 0, 0), (0, 0, 1, 0), (0, 0, 3, 0), (0, 0, 0, 1), (0, 0, 0, 7), (0, 1, 0, 0)]
SAME_CORE = sorted([(dx, dy) for dx in range(NX) for dy in range(NY) if dx or dy], key=lambda o: -(min(o[0], 4 - o[0]) + min(o[1], 4 - o[1])))
HOOK = 6
CHUNKS = 2
GROUPS = 8


def lane_bcast(v, lane):
    return jnp.broadcast_to(v[:, lane : lane + 1], (8, R))


def sub_bcast(v, sub):
    return jnp.broadcast_to(v[sub : sub + 1, :], (8, R))


def invert(A, between):
    lane = lax.broadcasted_iota(jnp.int32, (8, R), 1)
    sub = lax.broadcasted_iota(jnp.int32, (8, R), 0)
    t = [jnp.where(lane == sub + 8 * m, A[m], 0.0) for m in range(16)]
    down = [lax.rsqrt(jnp.sum(d, axis=1, keepdims=True)) for d in t]
    while len(t) > 1:
        t = [t[q] + t[q + 1] for q in range(0, len(t), 2)]
    across = lax.rsqrt(jnp.sum(t[0], axis=0, keepdims=True))
    A = [A[m] * across * down[m] for m in range(16)]
    for p in range(R // 16):
        between(p)
        l0 = 16 * p
        inside = (lane >= l0) & (lane < l0 + 16)
        own = [2 * p, 2 * p + 1]
        ahead = [m for m in (2 * p + 2, 2 * p + 3) if m < 16]
        c = [[lane_bcast(A[u], l0 + i) for u in own] for i in range(16)]
        rows = [jnp.where(inside, jnp.where(lane - l0 == sub + 8 * k, 1.0, 0.0), A[u]) for k, u in enumerate(own)]
        for i in range(0, 16, 2):
            v, s = i // 8, i % 8
            a, b = sub_bcast(c[i][v], s), sub_bcast(c[i + 1][v], s)
            d, e = sub_bcast(c[i][v], s + 1), sub_bcast(c[i + 1][v], s + 1)
            det = 1.0 / (a * e - b * d)
            g0 = [c[i][u] * e - c[i + 1][u] * d for u in range(2)]
            g1 = [c[i + 1][u] * a - c[i][u] * b for u in range(2)]
            g0[v] = jnp.where(sub == s, -e, jnp.where(sub == s + 1, d, g0[v]))
            g1[v] = jnp.where(sub == s, b, jnp.where(sub == s + 1, -a, g1[v]))
            hit = (sub == s) | (sub == s + 1)

            def step(t):
                r0, r1 = sub_bcast(t[v], s), sub_bcast(t[v], s + 1)
                kept = [jnp.where(hit, 0.0, t[u]) if u == v else t[u] for u in range(2)]
                return [kept[u] - (g0[u] * r0 + g1[u] * r1) * det for u in range(2)]

            for m in range(i + 2, 16):
                c[m] = step(c[m])
            rows = step(rows)
        new = list(A)
        for m in ahead:
            t = [lane_bcast(A[m], l0 + i) * sub_bcast(rows[i // 8], i % 8) for i in range(16)]
            while len(t) > 1:
                t = [t[q] + t[q + 1] for q in range(0, len(t), 2)]
            new[m] = jnp.where(inside, 0.0, A[m]) - t[0]
        padded = jnp.concatenate([rows[m - own[0]] if m in own else jnp.zeros((8, R), F32) for m in range(16)], axis=0)
        update = jnp.dot(jnp.concatenate(A, axis=0), padded, precision=HIGH, preferred_element_type=F32)
        for m in range(16):
            if m not in own and m not in ahead:
                new[m] = jnp.where(inside, 0.0, A[m]) - update[8 * m : 8 * m + 8]
        new[own[0]], new[own[1]] = rows
        A = new
    return [A[m] * across * down[m] for m in range(16)]


def kernel(
    base, opb, opc, db, dc, fb, fc, fa_out, gn_out,
    bv, cv, st_f, pass_f, rv_f, rv_d, part_g, y_g, z_g, ag_g, part_m, y_m, z_m, ag_m, mtm_v, inv,
    near, far, base_v, in_sem, op_sem, p_s, p_r, f_s, f_r, d_s, d_r, yg_s, yg_r, zg_s, zg_r, ag_s, ag_r, ym_s, ym_r, zm_s, zm_r, am_s, am_r, mt_s, mt_r,
):
    r, c = lax.axis_index("row"), lax.axis_index("col")
    x, core = r // 2, lax.rem(r, 2)
    z, y = c // NY, lax.rem(c, NY)

    def at_row(dx, dcore):
        return lax.rem(x + dx, NX) * 2 + lax.rem(core + dcore, NC)

    def at_col(dz, dy):
        return lax.rem(z + dz, NZ) * NY + lax.rem(y + dy, NY)

    def remote(src, dst, ss, rs, k, row, col):
        return pltpu.make_async_remote_copy(
            src_ref=src, dst_ref=dst, send_sem=ss.at[k], recv_sem=rs.at[k],
            device_id=(row, col), device_id_type=MESH)

    loads = []
    for g in range(CHUNKS):
        rows = pl.ds(64 // CHUNKS * g, 64 // CHUNKS)
        loads.append((pltpu.make_async_copy(opb.at[rows], bv.at[rows], op_sem.at[0, g]),
                      pltpu.make_async_copy(opc.at[rows], cv.at[rows], op_sem.at[1, g])))

    small = [pltpu.make_async_copy(src, dst, in_sem.at[k]) for k, (src, dst) in enumerate((
        (fb, st_f.at[0]), (fc, st_f.at[1]), (db, rv_d.at[x, core, :, pl.ds(0, 256)]),
        (dc, rv_d.at[x, core, :, pl.ds(256, 256)]), (base, base_v)))]
    barrier = pltpu.get_barrier_semaphore()
    for dx, dcore, dy, dz in GREETED:
        pl.semaphore_signal(barrier, inc=1, device_id=(at_row(dx, dcore), at_col(dz, dy)), device_id_type=MESH)
    for copy in small:
        copy.start()
    for copy in small:
        copy.wait()
    rv_f[x, core] = st_f[core]
    pass_f[x] = st_f[1 - core]
    pl.semaphore_wait(barrier, len(GREETED))

    def tell(sem, dz):
        for d in (dz, NZ - dz):
            pl.semaphore_signal(sem, inc=1, device_id=(r, at_col(d, 0)), device_id_type=MESH)

    sent = []
    pass_in, send_f, send_d = [], [], []
    for k, dx in enumerate((2, 1, 3)):
        pass_in.append(remote(st_f.at[1 - core], pass_f.at[x], p_s, p_r, k, at_row(dx, 0), c))
        pass_in[-1].start()
    for k, dx in enumerate((2, 1, 3)):
        send_d.append(remote(rv_d.at[x, core], rv_d.at[x, core], d_s, d_r, k, at_row(dx, 0), c))
        send_d[-1].start()
    for k, dx in enumerate((2, 1, 3)):
        send_f.append(remote(st_f.at[core], rv_f.at[x, core], f_s, f_r, k, at_row(dx, 0), c))
        send_f[-1].start()
    tell(near, 1)
    for pair in loads:
        for copy in pair:
            copy.start()

    for copy in pass_in:
        copy.wait_recv()
    over_f = remote(pass_f, rv_f.at[:, core], f_s, f_r, 3, at_row(0, 1), c)
    over_f.start()

    for copy in send_d:
        copy.wait_recv()
    over_d = remote(rv_d.at[:, core], rv_d.at[:, core], d_s, d_r, 3, at_row(0, 1), c)
    over_d.start()
    for copy in send_f + [over_f]:
        copy.wait_recv()
    mine = rv_f[x].reshape(32, 256)
    gram = lax.dot_general(mine, rv_f[...].reshape(R, 256), (((1,), (1,)), ((), ())),
                           precision=HIGH, preferred_element_type=F32)
    part_g[...] = gram.reshape(NY, 8, R)
    send_yg = []
    for dy in (2, 1, 3):
        send_yg.append(remote(part_g.at[lax.rem(y + dy, NY)], y_g.at[dy - 1], yg_s, yg_r, dy - 1, r, at_col(0, dy)))
        send_yg[-1].start()

    pl.semaphore_wait(near, 2)
    tell(far, 2)
    over_d.wait_recv()
    sent += pass_in + send_f + send_d + [over_f, over_d]
    lanes = lax.rem(lax.broadcasted_iota(jnp.int32, (R, 2 * R), 1), R)
    eye = lax.broadcasted_iota(jnp.int32, (R, 2 * R), 0) == lanes
    for g in range(GROUPS):
        if g % (GROUPS // CHUNKS) == 0:
            for copy in loads[g // (GROUPS // CHUNKS)]:
                copy.wait()
        d_b = rv_d[:, :, :, 0:256].reshape(R, 256)
        d_c = rv_d[:, :, :, 256:512].reshape(R, 256)
        found = []
        for i in range(8 * g, 8 * g + 8, 2):
            both = jnp.dot(d_b, jnp.concatenate([bv[i], bv[i + 1]], axis=1), preferred_element_type=F32)
            both = both + jnp.dot(d_c, jnp.concatenate([cv[i], cv[i + 1]], axis=1), preferred_element_type=F32)
            pair = jnp.sum(jnp.where(eye, both, 0.0), axis=0, keepdims=True)
            found += [pair[:, :R], pair[:, R:]]
        part_m[g // 2, pl.ds(8 * (g % 2), 8), :] = jnp.concatenate(found, axis=0)
    send_ym = []
    for dy in (2, 1, 3):
        send_ym.append(remote(part_m.at[lax.rem(y + dy, NY)], y_m.at[dy - 1], ym_s, ym_r, dy - 1, r, at_col(0, dy)))
        send_ym[-1].start()

    for copy in send_yg:
        copy.wait_recv()
    z_g[z] = (part_g[y] + y_g[0]) + (y_g[1] + y_g[2])
    pl.semaphore_wait(far, 2)
    send_zg = []
    for dz in (4, 3, 5, 2, 6, 1, 7):
        send_zg.append(remote(z_g.at[z], z_g.at[z], zg_s, zg_r, dz - 1, r, at_col(dz, 0)))
        send_zg[-1].start()

    for copy in send_ym:
        copy.wait_recv()
    z_m[z] = (part_m[y] + y_m[0]) + (y_m[1] + y_m[2])
    send_zm = []
    for dz in (4, 3, 5, 2, 6, 1, 7):
        send_zm.append(remote(z_m.at[z], z_m.at[z], zm_s, zm_r, dz - 1, r, at_col(dz, 0)))
        send_zm[-1].start()

    for copy in send_zg:
        copy.wait_recv()
    ag_g[x, core, y] = ((z_g[0] + z_g[1]) + (z_g[2] + z_g[3])) + ((z_g[4] + z_g[5]) + (z_g[6] + z_g[7]))
    send_ag = []
    for k, (dx, dy) in enumerate(SAME_CORE):
        send_ag.append(remote(ag_g.at[x, core, y], ag_g.at[x, core, y], ag_s, ag_r, k, at_row(dx, 0), at_col(0, dy)))
        send_ag[-1].start()

    for copy in send_zm:
        copy.wait_recv()
    summed = ((z_m[0] + z_m[1]) + (z_m[2] + z_m[3])) + ((z_m[4] + z_m[5]) + (z_m[6] + z_m[7]))
    ag_m[x, y] = base_v[pl.ds(pl.multiple_of(16 * y, 16), 16), :] + summed
    send_am = []
    for k, (dx, dy) in enumerate(SAME_CORE):
        send_am.append(remote(ag_m.at[x, y], ag_m.at[x, y], am_s, am_r, k, at_row(dx, 0), at_col(0, dy)))
        send_am[-1].start()

    for copy in sent + send_yg + send_zg + send_ym:
        copy.wait_send()
    for copy in send_ag:
        copy.wait_recv()
    over_g = remote(ag_g.at[:, core], ag_g.at[:, core], ag_s, ag_r, 15, at_row(0, 1), c)
    over_g.start()
    over_g.wait_recv()
    for copy in send_ag + send_zm:
        copy.wait_send()
    gathered = ag_g[...].reshape(NX, NC, 32, R)
    gram_b = gathered[:, 0].reshape(R, R)
    gram_c = gathered[:, 1].reshape(R, R) / K
    hadamard = gram_b / J * gram_c
    whole_sum = []

    def between(panel):
        if panel != HOOK:
            return
        for copy in send_am:
            copy.wait_recv()
        whole = ag_m[...].reshape(ROWS // 2, R)
        mtm_v[core] = lax.dot_general(whole, whole, (((0,), (0,)), ((), ())), precision=HIGH, preferred_element_type=F32)
        whole_sum.append(remote(mtm_v.at[core], mtm_v.at[core], mt_s, mt_r, 0, at_row(0, 1), c))
        whole_sum[0].start()

    blocks = invert([hadamard[8 * m : 8 * m + 8, :] for m in range(16)], between)
    for m in range(16):
        inv[8 * m : 8 * m + 8, :] = blocks[m]
    swap, = whole_sum
    swap.wait_recv()
    mtm = mtm_v[0] + mtm_v[1]
    inverse = inv[...]
    own = ag_m[x].reshape(64, R)
    both = jnp.dot(jnp.concatenate([mtm, own], axis=0), inverse, precision=HIGH, preferred_element_type=F32)
    half = both[:R]
    fa_out[...] = both[R:]
    gram_a = jnp.dot(inverse, half, precision=HIGH, preferred_element_type=F32)
    gn_out[...] = gram_a / ROWS * gram_c

    for copy in send_am + [swap, over_g]:
        copy.wait_send()


def deliver(fa, gn, fa_out, gn_out, sem):
    copies = [pltpu.make_async_copy(src, dst, sem.at[k]) for k, (src, dst) in enumerate(((fa, fa_out), (gn, gn_out)))]
    for copy in copies:
        copy.start()
    for copy in copies:
        copy.wait()


def shards(base_mttkrp, operator_b, operator_c, delta_b, delta_c, factor_b, factor_c):
    args = (base_mttkrp, operator_b, operator_c, delta_b.T, delta_c.T, factor_b.T, factor_c.T)
    vmem = pl.BlockSpec(memory_space=pltpu.VMEM)
    hbm = pl.BlockSpec(memory_space=pltpu.HBM)

    def sems(*counts):
        return [pltpu.SemaphoreType.DMA((n,)) for n in counts for _ in range(2)]

    solved = pl.pallas_call(
        kernel,
        out_shape=(pltpu.VMEM((64, R), F32), pltpu.VMEM((R, R), F32)),
        in_specs=[hbm] * 7,
        out_specs=(vmem, vmem),
        scratch_shapes=[
            pltpu.VMEM((64, 256, R), BF16),
            pltpu.VMEM((64, 256, R), BF16),
            pltpu.VMEM((2, 16, 256), F32),
            pltpu.VMEM((NX, 16, 256), F32),
            pltpu.VMEM((NX, NC, 16, 256), F32),
            pltpu.VMEM((NX, NC, 16, 512), BF16),
            pltpu.VMEM((NY, 8, R), F32),
            pltpu.VMEM((NY - 1, 8, R), F32),
            pltpu.VMEM((NZ, 8, R), F32),
            pltpu.VMEM((NX, NC, NY, 8, R), F32),
            pltpu.VMEM((NY, 16, R), F32),
            pltpu.VMEM((NY - 1, 16, R), F32),
            pltpu.VMEM((NZ, 16, R), F32),
            pltpu.VMEM((NX, NY, 16, R), F32),
            pltpu.VMEM((NC, R, R), F32),
            pltpu.VMEM((R, R), F32),
            pltpu.SemaphoreType.REGULAR,
            pltpu.SemaphoreType.REGULAR,
            pltpu.VMEM((64, R), F32),
            pltpu.SemaphoreType.DMA((5,)),
            pltpu.SemaphoreType.DMA((2, CHUNKS)),
        ] + sems(3, 4, 4, 3, 7, 16, 3, 7, 15, 1),
        compiler_params=pltpu.CompilerParams(
            collective_id=0, has_side_effects=True, vmem_limit_bytes=40 * 2**20),
        name="update",
    )(*(pltpu.with_memory_space_constraint(a, pltpu.HBM) for a in args))
    return pl.pallas_call(
        deliver,
        out_shape=(jax.ShapeDtypeStruct((64, R), F32), jax.ShapeDtypeStruct((R, R), F32)),
        in_specs=[vmem] * 2,
        out_specs=(hbm, hbm),
        scratch_shapes=[pltpu.SemaphoreType.DMA((2,))],
        name="deliver",
    )(*(pltpu.with_memory_space_constraint(a, pltpu.VMEM) for a in solved))


def solution(mesh):
    return jax.shard_map(
        shards,
        mesh=mesh,
        in_specs=(
            P("row", None),
            P("row", "col", None),
            P("row", "col", None),
            P("col", "row"),
            P("col", "row"),
            P("col", "row"),
            P("col", "row"),
        ),
        out_specs=(P("row", None), P()),
        check_vma=False,
    )
```

```python
import functools

import jax
import jax.numpy as jnp
from jax import lax
from jax.experimental import pallas as pl
from jax.experimental.pallas import tpu as pltpu
from jax.sharding import PartitionSpec as P

J = 8192
K = 8192
ROWS = 512
R = 128
F32 = jnp.float32
BF16 = jnp.bfloat16
HIGH = lax.Precision.HIGHEST
MESH = pl.DeviceIdType.MESH

NX, NC, NY, NZ = 4, 2, 4, 8
XY_OFFS = [(dx, dc, dy) for dy in range(NY) for dx in range(NX) for dc in range(NC) if dx or dc or dy]
GREETED = [(2, 0, 0, 0), (0, 0, 2, 0), (1, 0, 0, 0), (3, 0, 0, 0), (0, 0, 1, 0), (0, 0, 3, 0), (0, 0, 0, 1), (0, 0, 0, 7), (0, 1, 0, 0)]
SAME_CORE = sorted([(dx, dy) for dx in range(NX) for dy in range(NY) if dx or dy], key=lambda o: -(min(o[0], 4 - o[0]) + min(o[1], 4 - o[1])))
HOOK = 6
CHUNKS = 2
GROUPS = 8


def lane_bcast(v, lane):
    return jnp.broadcast_to(v[:, lane : lane + 1], (8, R))


def sub_bcast(v, sub):
    return jnp.broadcast_to(v[sub : sub + 1, :], (8, R))


def invert(A, between):
    lane = lax.broadcasted_iota(jnp.int32, (8, R), 1)
    sub = lax.broadcasted_iota(jnp.int32, (8, R), 0)
    t = [jnp.where(lane == sub + 8 * m, A[m], 0.0) for m in range(16)]
    down = [lax.rsqrt(jnp.sum(d, axis=1, keepdims=True)) for d in t]
    while len(t) > 1:
        t = [t[q] + t[q + 1] for q in range(0, len(t), 2)]
    across = lax.rsqrt(jnp.sum(t[0], axis=0, keepdims=True))
    A = [A[m] * across * down[m] for m in range(16)]
    for p in range(R // 16):
        between(p)
        l0 = 16 * p
        inside = (lane >= l0) & (lane < l0 + 16)
        own = [2 * p, 2 * p + 1]
        ahead = [m for m in (2 * p + 2, 2 * p + 3) if m < 16]
        c = [[lane_bcast(A[u], l0 + i) for u in own] for i in range(16)]
        rows = [jnp.where(inside, jnp.where(lane - l0 == sub + 8 * k, 1.0, 0.0), A[u]) for k, u in enumerate(own)]
        for i in range(0, 16, 2):
            v, s = i // 8, i % 8
            a, b = sub_bcast(c[i][v], s), sub_bcast(c[i + 1][v], s)
            d, e = sub_bcast(c[i][v], s + 1), sub_bcast(c[i + 1][v], s + 1)
            det = 1.0 / (a * e - b * d)
            g0 = [c[i][u] * e - c[i + 1][u] * d for u in range(2)]
            g1 = [c[i + 1][u] * a - c[i][u] * b for u in range(2)]
            g0[v] = jnp.where(sub == s, -e, jnp.where(sub == s + 1, d, g0[v]))
            g1[v] = jnp.where(sub == s, b, jnp.where(sub == s + 1, -a, g1[v]))
            hit = (sub == s) | (sub == s + 1)

            def step(t):
                r0, r1 = sub_bcast(t[v], s), sub_bcast(t[v], s + 1)
                kept = [jnp.where(hit, 0.0, t[u]) if u == v else t[u] for u in range(2)]
                return [kept[u] - (g0[u] * r0 + g1[u] * r1) * det for u in range(2)]

            for m in range(i + 2, 16):
                c[m] = step(c[m])
            rows = step(rows)
        new = list(A)
        for m in ahead:
            t = [lane_bcast(A[m], l0 + i) * sub_bcast(rows[i // 8], i % 8) for i in range(16)]
            while len(t) > 1:
                t = [t[q] + t[q + 1] for q in range(0, len(t), 2)]
            new[m] = jnp.where(inside, 0.0, A[m]) - t[0]
        padded = jnp.concatenate([rows[m - own[0]] if m in own else jnp.zeros((8, R), F32) for m in range(16)], axis=0)
        update = jnp.dot(jnp.concatenate(A, axis=0), padded, precision=HIGH, preferred_element_type=F32)
        for m in range(16):
            if m not in own and m not in ahead:
                new[m] = jnp.where(inside, 0.0, A[m]) - update[8 * m : 8 * m + 8]
        new[own[0]], new[own[1]] = rows
        A = new
    return [A[m] * across * down[m] for m in range(16)]


def kernel(
    base, opb, opc, db, dc, fb, fc, fa_out, gn_out,
    bv, cv, st_f, pass_f, rv_f, rv_d, part_g, y_g, z_g, ag_g, part_m, y_m, z_m, ag_m, mtm_v, inv,
    near, far, base_v, in_sem, op_sem, p_s, p_r, f_s, f_r, d_s, d_r, yg_s, yg_r, zg_s, zg_r, ag_s, ag_r, ym_s, ym_r, zm_s, zm_r, am_s, am_r, mt_s, mt_r,
):
    r, c = lax.axis_index("row"), lax.axis_index("col")
    x, core = r // 2, lax.rem(r, 2)
    z, y = c // NY, lax.rem(c, NY)

    def at_row(dx, dcore):
        return lax.rem(x + dx, NX) * 2 + lax.rem(core + dcore, NC)

    def at_col(dz, dy):
        return lax.rem(z + dz, NZ) * NY + lax.rem(y + dy, NY)

    def remote(src, dst, ss, rs, k, row, col):
        return pltpu.make_async_remote_copy(
            src_ref=src, dst_ref=dst, send_sem=ss.at[k], recv_sem=rs.at[k],
            device_id=(row, col), device_id_type=MESH)

    loads = []
    for g in range(CHUNKS):
        rows = pl.ds(64 // CHUNKS * g, 64 // CHUNKS)
        loads.append((pltpu.make_async_copy(opb.at[rows], bv.at[rows], op_sem.at[0, g]),
                      pltpu.make_async_copy(opc.at[rows], cv.at[rows], op_sem.at[1, g])))

    small = [pltpu.make_async_copy(src, dst, in_sem.at[k]) for k, (src, dst) in enumerate((
        (fb, st_f.at[0]), (fc, st_f.at[1]), (db, rv_d.at[x, core, :, pl.ds(0, 256)]),
        (dc, rv_d.at[x, core, :, pl.ds(256, 256)]), (base, base_v)))]
    barrier = pltpu.get_barrier_semaphore()
    for dx, dcore, dy, dz in GREETED:
        pl.semaphore_signal(barrier, inc=1, device_id=(at_row(dx, dcore), at_col(dz, dy)), device_id_type=MESH)
    for copy in small:
        copy.start()
    for copy in small[:4]:
        copy.wait()
    rv_f[x, core] = st_f[core]
    pass_f[x] = st_f[1 - core]
    pl.semaphore_wait(barrier, len(GREETED))

    def tell(sem, dz):
        for d in (dz, NZ - dz):
            pl.semaphore_signal(sem, inc=1, device_id=(r, at_col(d, 0)), device_id_type=MESH)

    sent = []
    pass_in, send_f, send_d = [], [], []
    for k, dx in enumerate((2, 1, 3)):
        pass_in.append(remote(st_f.at[1 - core], pass_f.at[x], p_s, p_r, k, at_row(dx, 0), c))
        pass_in[-1].start()
    for k, dx in enumerate((2, 1, 3)):
        send_d.append(remote(rv_d.at[x, core], rv_d.at[x, core], d_s, d_r, k, at_row(dx, 0), c))
        send_d[-1].start()
    for k, dx in enumerate((2, 1, 3)):
        send_f.append(remote(st_f.at[core], rv_f.at[x, core], f_s, f_r, k, at_row(dx, 0), c))
        send_f[-1].start()
    tell(near, 1)
    for pair in loads:
        for copy in pair:
            copy.start()

    for copy in pass_in:
        copy.wait_recv()
    over_f = remote(pass_f, rv_f.at[:, core], f_s, f_r, 3, at_row(0, 1), c)
    over_f.start()

    for copy in send_d:
        copy.wait_recv()
    over_d = remote(rv_d.at[:, core], rv_d.at[:, core], d_s, d_r, 3, at_row(0, 1), c)
    over_d.start()
    for copy in send_f + [over_f]:
        copy.wait_recv()
    mine = rv_f[x].reshape(32, 256)
    gram = lax.dot_general(mine, rv_f[...].reshape(R, 256), (((1,), (1,)), ((), ())),
                           precision=HIGH, preferred_element_type=F32)
    part_g[...] = gram.reshape(NY, 8, R)
    send_yg = []
    for dy in (2, 1, 3):
        send_yg.append(remote(part_g.at[lax.rem(y + dy, NY)], y_g.at[dy - 1], yg_s, yg_r, dy - 1, r, at_col(0, dy)))
        send_yg[-1].start()

    pl.semaphore_wait(near, 2)
    tell(far, 2)
    over_d.wait_recv()
    sent += pass_in + send_f + send_d + [over_f, over_d]
    lanes = lax.rem(lax.broadcasted_iota(jnp.int32, (R, 2 * R), 1), R)
    eye = lax.broadcasted_iota(jnp.int32, (R, 2 * R), 0) == lanes
    for g in range(GROUPS):
        if g % (GROUPS // CHUNKS) == 0:
            for copy in loads[g // (GROUPS // CHUNKS)]:
                copy.wait()
        d_b = rv_d[:, :, :, 0:256].reshape(R, 256)
        d_c = rv_d[:, :, :, 256:512].reshape(R, 256)
        found = []
        for i in range(8 * g, 8 * g + 8, 2):
            both = jnp.dot(d_b, jnp.concatenate([bv[i], bv[i + 1]], axis=1), preferred_element_type=F32)
            both = both + jnp.dot(d_c, jnp.concatenate([cv[i], cv[i + 1]], axis=1), preferred_element_type=F32)
            pair = jnp.sum(jnp.where(eye, both, 0.0), axis=0, keepdims=True)
            found += [pair[:, :R], pair[:, R:]]
        part_m[g // 2, pl.ds(8 * (g % 2), 8), :] = jnp.concatenate(found, axis=0)
    send_ym = []
    for dy in (2, 1, 3):
        send_ym.append(remote(part_m.at[lax.rem(y + dy, NY)], y_m.at[dy - 1], ym_s, ym_r, dy - 1, r, at_col(0, dy)))
        send_ym[-1].start()

    for copy in send_yg:
        copy.wait_recv()
    z_g[z] = (part_g[y] + y_g[0]) + (y_g[1] + y_g[2])
    pl.semaphore_wait(far, 2)
    send_zg = []
    for dz in (4, 3, 5, 2, 6, 1, 7):
        send_zg.append(remote(z_g.at[z], z_g.at[z], zg_s, zg_r, dz - 1, r, at_col(dz, 0)))
        send_zg[-1].start()

    for copy in send_ym:
        copy.wait_recv()
    z_m[z] = (part_m[y] + y_m[0]) + (y_m[1] + y_m[2])
    send_zm = []
    for dz in (4, 3, 5, 2, 6, 1, 7):
        send_zm.append(remote(z_m.at[z], z_m.at[z], zm_s, zm_r, dz - 1, r, at_col(dz, 0)))
        send_zm[-1].start()

    for copy in send_zg:
        copy.wait_recv()
    ag_g[x, core, y] = ((z_g[0] + z_g[1]) + (z_g[2] + z_g[3])) + ((z_g[4] + z_g[5]) + (z_g[6] + z_g[7]))
    send_ag = []
    for k, (dx, dy) in enumerate(SAME_CORE):
        send_ag.append(remote(ag_g.at[x, core, y], ag_g.at[x, core, y], ag_s, ag_r, k, at_row(dx, 0), at_col(0, dy)))
        send_ag[-1].start()

    for copy in send_zm:
        copy.wait_recv()
    summed = ((z_m[0] + z_m[1]) + (z_m[2] + z_m[3])) + ((z_m[4] + z_m[5]) + (z_m[6] + z_m[7]))
    small[4].wait()
    ag_m[x, y] = base_v[pl.ds(pl.multiple_of(16 * y, 16), 16), :] + summed
    send_am = []
    for k, (dx, dy) in enumerate(SAME_CORE):
        send_am.append(remote(ag_m.at[x, y], ag_m.at[x, y], am_s, am_r, k, at_row(dx, 0), at_col(0, dy)))
        send_am[-1].start()

    for copy in sent + send_yg + send_zg + send_ym:
        copy.wait_send()
    for copy in send_ag:
        copy.wait_recv()
    over_g = remote(ag_g.at[:, core], ag_g.at[:, core], ag_s, ag_r, 15, at_row(0, 1), c)
    over_g.start()
    over_g.wait_recv()
    for copy in send_ag + send_zm:
        copy.wait_send()
    gathered = ag_g[...].reshape(NX, NC, 32, R)
    gram_b = gathered[:, 0].reshape(R, R)
    gram_c = gathered[:, 1].reshape(R, R) / K
    hadamard = gram_b / J * gram_c
    whole_sum = []

    def between(panel):
        if panel != HOOK:
            return
        for copy in send_am:
            copy.wait_recv()
        whole = ag_m[...].reshape(ROWS // 2, R)
        mtm_v[core] = lax.dot_general(whole, whole, (((0,), (0,)), ((), ())), precision=HIGH, preferred_element_type=F32)
        whole_sum.append(remote(mtm_v.at[core], mtm_v.at[core], mt_s, mt_r, 0, at_row(0, 1), c))
        whole_sum[0].start()

    blocks = invert([hadamard[8 * m : 8 * m + 8, :] for m in range(16)], between)
    for m in range(16):
        inv[8 * m : 8 * m + 8, :] = blocks[m]
    swap, = whole_sum
    swap.wait_recv()
    mtm = mtm_v[0] + mtm_v[1]
    inverse = inv[...]
    own = ag_m[x].reshape(64, R)
    both = jnp.dot(jnp.concatenate([mtm, own], axis=0), inverse, precision=HIGH, preferred_element_type=F32)
    half = both[:R]
    fa_out[...] = both[R:]
    gram_a = jnp.dot(inverse, half, precision=HIGH, preferred_element_type=F32)
    gn_out[...] = gram_a / ROWS * gram_c

    for copy in send_am + [swap, over_g]:
        copy.wait_send()


def deliver(fa, gn, fa_out, gn_out, sem):
    copies = [pltpu.make_async_copy(src, dst, sem.at[k]) for k, (src, dst) in enumerate(((fa, fa_out), (gn, gn_out)))]
    for copy in copies:
        copy.start()
    for copy in copies:
        copy.wait()


def shards(base_mttkrp, operator_b, operator_c, delta_b, delta_c, factor_b, factor_c):
    args = (base_mttkrp, operator_b, operator_c, delta_b.T, delta_c.T, factor_b.T, factor_c.T)
    vmem = pl.BlockSpec(memory_space=pltpu.VMEM)
    hbm = pl.BlockSpec(memory_space=pltpu.HBM)

    def sems(*counts):
        return [pltpu.SemaphoreType.DMA((n,)) for n in counts for _ in range(2)]

    solved = pl.pallas_call(
        kernel,
        out_shape=(pltpu.VMEM((64, R), F32), pltpu.VMEM((R, R), F32)),
        in_specs=[hbm] * 7,
        out_specs=(vmem, vmem),
        scratch_shapes=[
            pltpu.VMEM((64, 256, R), BF16),
            pltpu.VMEM((64, 256, R), BF16),
            pltpu.VMEM((2, 16, 256), F32),
            pltpu.VMEM((NX, 16, 256), F32),
            pltpu.VMEM((NX, NC, 16, 256), F32),
            pltpu.VMEM((NX, NC, 16, 512), BF16),
            pltpu.VMEM((NY, 8, R), F32),
            pltpu.VMEM((NY - 1, 8, R), F32),
            pltpu.VMEM((NZ, 8, R), F32),
            pltpu.VMEM((NX, NC, NY, 8, R), F32),
            pltpu.VMEM((NY, 16, R), F32),
            pltpu.VMEM((NY - 1, 16, R), F32),
            pltpu.VMEM((NZ, 16, R), F32),
            pltpu.VMEM((NX, NY, 16, R), F32),
            pltpu.VMEM((NC, R, R), F32),
            pltpu.VMEM((R, R), F32),
            pltpu.SemaphoreType.REGULAR,
            pltpu.SemaphoreType.REGULAR,
            pltpu.VMEM((64, R), F32),
            pltpu.SemaphoreType.DMA((5,)),
            pltpu.SemaphoreType.DMA((2, CHUNKS)),
        ] + sems(3, 4, 4, 3, 7, 16, 3, 7, 15, 1),
        compiler_params=pltpu.CompilerParams(
            collective_id=0, has_side_effects=True, vmem_limit_bytes=40 * 2**20),
        name="update",
    )(*(pltpu.with_memory_space_constraint(a, pltpu.HBM) for a in args))
    return pl.pallas_call(
        deliver,
        out_shape=(jax.ShapeDtypeStruct((64, R), F32), jax.ShapeDtypeStruct((R, R), F32)),
        in_specs=[vmem] * 2,
        out_specs=(hbm, hbm),
        scratch_shapes=[pltpu.SemaphoreType.DMA((2,))],
        name="deliver",
    )(*(pltpu.with_memory_space_constraint(a, pltpu.VMEM) for a in solved))


def solution(mesh):
    return jax.shard_map(
        shards,
        mesh=mesh,
        in_specs=(
            P("row", None),
            P("row", "col", None),
            P("row", "col", None),
            P("col", "row"),
            P("col", "row"),
            P("col", "row"),
            P("col", "row"),
        ),
        out_specs=(P("row", None), P()),
        check_vma=False,
    )
```
